256 devices in a mesh: gx: 32 (over z_lo, y, core), gy: 8 (over z_hi, x).
Axes of the slice: x: 4, y: 4, z: 8 (z_hi: 2, z_lo: 4; z = z_hi * 4 + z_lo), core: 2. Of those that a mesh axis runs over, the one named last changes fastest.
Arguments:
- child_state: float32 [5, 32, 512, 1024], P(None, None, 'gx', 'gy'), may hold values from -6 to 6
- cotangent: float32 [5, 32, 512, 1024], P(None, None, 'gx', 'gy'), may hold values from -6 to 6
- diffusivity: float32 [32, 512, 1024], P(None, 'gx', 'gy'), may hold values from 0.01 to 0.16
- field_mix: float32 [5, 5], replicated, may hold values from -2.5 to 2.5
- parent_we: float32 [2, 5, 128, 1024], P(None, None, 'gx', 'gy'), may hold values from -6 to 6
- parent_sn: float32 [2, 5, 128, 512], P(None, None, 'gy', 'gx'), may hold values from -6 to 6
- terrain_we: int32 [2, 1024], P(None, 'gy'), may hold values from 0 to 96, as said below
- terrain_sn: int32 [2, 512], P(None, 'gx'), may hold values from 0 to 96, as said below
- relax_width: int32 [1], replicated, may hold values from 4 to 15
Outputs:
- child_final: float32 [5, 32, 512, 1024], P(None, None, 'gx', 'gy')
- grad_state: float32 [5, 32, 512, 1024], P(None, None, 'gx', 'gy')
- grad_we: float32 [2, 5, 128, 1024], P(None, None, 'gx', 'gy')
- grad_sn: float32 [2, 5, 128, 512], P(None, None, 'gy', 'gx')
The draws below stay inside these ranges and needn't reach their ends.
Inputs may be any that keep to these rules, and one draw needn't show every extreme that they name: `terrain_we`: on each edge some column has the largest value 128 - 32. `terrain_sn`: on each edge some column has the largest value 128 - 32.
All inputs are finite; a program needn't handle non-finite values.
Results may differ from the reference program's by a relative error of at most 0.000084.
Values sent between devices are 32-bit elements; how exact they have to be, the bound alone decides.
A program may use at most 128 MiB of HBM per device.

```python
import math
import jax
import jax.numpy as jnp
from jax import lax

F = 5
KC = 32
KP = 128
CX = 16
NX = 512
NY = 1024


def terrain_columns(key, count):
    first_key, second_key = jax.random.split(key)
    heights = jax.random.randint(first_key, (2, count), 0, KP - KC + 1, dtype=jnp.int32)
    chosen = jax.random.randint(second_key, (2,), 0, count, dtype=jnp.int32)
    column = jnp.arange(count, dtype=jnp.int32)
    return jnp.where(column[None, :] == chosen[:, None], KP - KC, heights).astype(jnp.int32)


def draw_terrain_we(key, part):
    key = jax.random.fold_in(key, 11)
    return terrain_columns(key, NY)


def draw_terrain_sn(key, part):
    key = jax.random.fold_in(key, 23)
    return terrain_columns(key, NX)


def block_scale(rng, shape, shards, low, high):
    factor_of = 1.0
    for axis_at, shards_of in shards:
        steps = jax.random.uniform(jax.random.fold_in(jax.random.fold_in(rng, 6), axis_at), (shards_of,), jnp.float32, low / len(shards), high / len(shards))
        factor_of = factor_of * jnp.repeat(jnp.exp(steps), shape[axis_at] // shards_of).reshape((-1,) + (1,) * (len(shape) - 1 - axis_at))
    return factor_of


def centred(stream_key, shape, width, reach, cuts=(), held_as=jnp.bfloat16):
    factor_of = block_scale(stream_key, shape, cuts, -0.22, 0.18) if cuts else 1.0
    entries = jax.random.normal(stream_key, shape, jnp.float32) * width * factor_of
    return jnp.minimum(jnp.maximum(entries, -reach), reach).astype(held_as)


def setup_inputs(seed: int = 0) -> dict:
    streams_of = jax.random.split(jax.random.key(seed), 10)
    return {
        "child_state": centred(streams_of[0], (F, KC, NX, NY), 1.0, 6.0, ((2, 32), (3, 8)), jnp.float32),
        "cotangent": centred(streams_of[1], (F, KC, NX, NY), 1.0, 6.0, ((2, 32), (3, 8)), jnp.float32),
        "diffusivity": jnp.clip(jnp.exp(math.log(0.16) - 2.7725887 * jax.random.uniform(streams_of[2], (KC, NX, NY), jnp.float32) ** block_scale(streams_of[2], (KC, NX, NY), ((1, 32), (2, 8)), -0.2, 0.2)), 0.01, 0.16),
        "field_mix": centred(streams_of[3], (F, F), F ** -0.5, 2.5, (), jnp.float32),
        "parent_we": centred(streams_of[4], (2, F, KP, NY), 1.0, 6.0, ((2, 32), (3, 8)), jnp.float32),
        "parent_sn": centred(streams_of[5], (2, F, KP, NX), 1.0, 6.0, ((2, 8), (3, 32)), jnp.float32),
        "terrain_we": draw_terrain_we(jax.random.fold_in(streams_of[9], 71), 0),
        "terrain_sn": draw_terrain_sn(jax.random.fold_in(streams_of[9], 71), 0),
        "relax_width": jax.random.randint(streams_of[8], (1,), 4, CX).astype(jnp.int32),
    }


near_weight = 4.0 / 3.0
far_weight = -1.0 / 12.0
coupling = 0.25
highest = lax.Precision.HIGHEST


def laplace(padded):
    centre_cell = padded[..., 2:-2, 2:-2]
    summed = near_weight * (padded[..., 3:-1, 2:-2] + padded[..., 1:-3, 2:-2] + padded[..., 2:-2, 3:-1] + padded[..., 2:-2, 1:-3])
    summed = summed + far_weight * (padded[..., 4:, 2:-2] + padded[..., :-4, 2:-2] + padded[..., 2:-2, 4:] + padded[..., 2:-2, :-4])
    return summed - 5.0 * centre_cell


def zone_ramp(position, length, zone_width):
    distance = jnp.minimum(position, length - 1 - position)
    return jnp.maximum(zone_width - distance, 0).astype(jnp.float32) / (zone_width + 1).astype(jnp.float32)


def level_weights(terrain, first_level, level_count, child_count):
    child_level = jnp.arange(child_count, dtype=jnp.int32)
    base_level = terrain[:, None, :] + child_level[None, :, None]
    parent = first_level + jnp.arange(level_count, dtype=jnp.int32)
    return (parent[None, None, :, None] == base_level[:, :, None, :]).astype(jnp.float32)


def reference(child_state, cotangent, diffusivity, field_mix, parent_we, parent_sn, terrain_we, terrain_sn, relax_width):
    zone_width = relax_width[0]
    position_x = jnp.arange(NX, dtype=jnp.int32)
    position_y = jnp.arange(NY, dtype=jnp.int32)
    ramp_x = zone_ramp(position_x, NX, zone_width)[:, None]
    ramp_y = zone_ramp(position_y, NY, zone_width)[None, :]
    west_side = (position_x < NX // 2)[:, None]
    south_side = (position_y < NY // 2)[None, :]
    weights_we = level_weights(terrain_we, 0, KP, KC)
    weights_sn = level_weights(terrain_sn, 0, KP, KC)
    bound_we = jnp.einsum("eflc,eklc->efkc", parent_we, weights_we, precision=highest)
    bound_sn = jnp.einsum("eflc,eklc->efkc", parent_sn, weights_sn, precision=highest)

    def per_level(level_items):
        fields_now, adjoint, conduct, edge_we, edge_sn = level_items
        edge_x = jnp.where(west_side[None], edge_we[0][:, None, :], edge_we[1][:, None, :])
        edge_y = jnp.where(south_side[None], edge_sn[0][:, :, None], edge_sn[1][:, :, None])

        def advance(values):
            padded = jnp.pad(values, ((0, 0), (2, 2), (2, 2)))
            stepped = values + conduct * laplace(padded) + coupling * jnp.einsum("fg,gxy->fxy", field_mix, values, precision=highest)
            across = (1.0 - ramp_x) * stepped + ramp_x * edge_x
            return (1.0 - ramp_y) * across + ramp_y * edge_y

        def retreat(incoming):
            pulled = (1.0 - ramp_y) * (1.0 - ramp_x) * incoming
            padded = jnp.pad(conduct * pulled, ((0, 0), (2, 2), (2, 2)))
            return pulled + laplace(padded) + coupling * jnp.einsum("gf,gxy->fxy", field_mix, pulled, precision=highest)

        final_fields = advance(advance(fields_now))
        middle = retreat(adjoint)
        earliest = retreat(middle)
        carried = adjoint + middle
        push_x = (1.0 - ramp_y) * ramp_x * carried
        push_y = ramp_y * carried
        d_we = jnp.stack([jnp.sum(jnp.where(west_side, push_x, 0.0), axis=1), jnp.sum(jnp.where(west_side, 0.0, push_x), axis=1)])
        d_sn = jnp.stack([jnp.sum(jnp.where(south_side, push_y, 0.0), axis=2), jnp.sum(jnp.where(south_side, 0.0, push_y), axis=2)])
        return final_fields, earliest, d_we, d_sn

    mapped = lax.map(per_level, (child_state.transpose(1, 0, 2, 3), cotangent.transpose(1, 0, 2, 3), diffusivity, bound_we.transpose(2, 0, 1, 3), bound_sn.transpose(2, 0, 1, 3)))
    child_final = mapped[0].transpose(1, 0, 2, 3)
    grad_state = mapped[1].transpose(1, 0, 2, 3)
    d_we = mapped[2].transpose(1, 2, 0, 3)
    d_sn = mapped[3].transpose(1, 2, 0, 3)
    grad_we = jnp.einsum("efkc,eklc->eflc", d_we, weights_we, precision=highest)
    grad_sn = jnp.einsum("efkc,eklc->eflc", d_sn, weights_sn, precision=highest)
    return (child_final, grad_state, grad_we, grad_sn)
```

```python
import functools

import jax
import jax.numpy as jnp
from jax import lax
from jax.experimental import pallas as pl
from jax.experimental.pallas import tpu as pltpu
from jax.sharding import PartitionSpec as P

MESH = pl.DeviceIdType.MESH
F, KC, KP, CX, CY = 5, 32, 128, 16, 128
G = KC // 8
f32 = jnp.float32

L_COT, L_DIF, L_STATE, L_TWE, L_TSN, L_PWE, L_PSN, L_GWE, L_GSN, L_GRAD, L_FINAL, L_MIX, L_RW = range(13)
R_Q1, R_U0, R_Q2, R_U1 = range(4)
LEFT, RIGHT, DOWN, UP = range(4)
S_PWE, S_PSN = 16, 18
S_GWE, S_GSN = 20, 22
NSEM = 24


def tile(shape_dim):
    return lax.broadcasted_iota(jnp.int32, (8, CY), shape_dim)


def kernel(
    nx, ny,
    state, cot, dif, mix_in, pwe_in, psn_in, twe_in, tsn_in, rw_in,
    final, grad, gwe, gsn,
    u0, u1, q1, q2, a0, mid, out_f, out_g, edge, dp, dz, ztab,
    pwe, psn, bwe, bsn, gw, gs, packs, heard, own, halo, twe, tsn, mix, rw,
    loc, snd, rcv,
):
    gx, gy = lax.axis_index("gx"), lax.axis_index("gy")
    lane = tile(1)
    low2, high2, quad = lane < 2, lane >= CY - 2, lax.rem(lane, 4) < 2
    ends2 = low2 | high2
    x_end, y_end = (gx == 0) | (gx == nx - 1), (gy == 0) | (gy == ny - 1)

    def here(src, dst, sem):
        return pltpu.make_async_copy(src, dst, loc.at[sem])

    def whole(ref, sems, i):
        return pltpu.make_async_copy(ref, ref, sems.at[i])

    for x in range(CX):
        here(cot.at[:, :, x, :], a0.at[:, x], L_COT).start()
        here(dif.at[:, x, :], dp.at[x], L_DIF).start()
    here(twe_in, twe, L_TWE).start()
    here(tsn_in, tsn, L_TSN).start()
    here(mix_in, mix, L_MIX).start()
    here(rw_in, rw, L_RW).start()
    for x in range(CX):
        here(state.at[:, :, x, :], u0.at[:, x + 2], L_STATE).start()

    barrier = pltpu.get_barrier_semaphore()

    def greet(cond, to):
        @pl.when(cond)
        def _():
            pl.semaphore_signal(barrier, inc=1, device_id=to, device_id_type=MESH)

    def count(*conds):
        return sum(c.astype(jnp.int32) for c in conds)

    near = [(gx > 0, {"gx": gx - 1}), (gx < nx - 1, {"gx": gx + 1}), (gy > 0, {"gy": gy - 1}), (gy < ny - 1, {"gy": gy + 1})]
    for cond, to in near:
        greet(cond, to)
    for axis, at, n in (("gx", gx, nx), ("gy", gy, ny)):
        for e in (0, n - 1):
            @pl.when(at == e)
            def _(axis=axis, e=e, n=n):
                def one(i, c):
                    to = i + 1 if e == 0 else i
                    pl.semaphore_signal(barrier, inc=1, device_id={axis: to}, device_id_type=MESH)
                    return c
                lax.fori_loop(0, n - 1, one, 0)
            greet(at != e, {axis: jnp.int32(e)})
    wanted = count(*[c for c, _ in near])
    for at, n in ((gx, nx), (gy, ny)):
        for e in (0, n - 1):
            wanted = wanted + jnp.where(at == e, n - 1, 1)
    pl.semaphore_wait(barrier, wanted)

    def send(src, dst, i, j, to):
        return pltpu.make_async_remote_copy(src_ref=src, dst_ref=dst, send_sem=snd.at[i], recv_sem=rcv.at[j], device_id=to, device_id_type=MESH)

    @pl.when(gx > 0)
    def _():
        for i in range(2):
            send(state.at[:, :, i, :], u0.at[:, CX + 2 + i], 4 * R_U0 + LEFT, 4 * R_U0 + LEFT, {"gx": gx - 1}).start()

    @pl.when(gx < nx - 1)
    def _():
        for i in range(2):
            send(state.at[:, :, CX - 2 + i, :], u0.at[:, i], 4 * R_U0 + RIGHT, 4 * R_U0 + RIGHT, {"gx": gx + 1}).start()

    gather = (("gx", gx, nx, pwe_in, pwe, S_PWE, L_PWE), ("gy", gy, ny, psn_in, psn, S_PSN, L_PSN))
    for axis, at, n, src, dst, s, l in gather:
        for e, end in ((0, 0), (1, n - 1)):
            @pl.when(at != end)
            def _():
                send(src.at[e], dst.at[at], s + e, s, {axis: jnp.int32(end)}).start()

            @pl.when(at == end)
            def _():
                here(src.at[e], dst.at[end], l).start()

    zero = jnp.zeros((8, CY), f32)

    def clear(cond, ref, cols):
        @pl.when(cond)
        def _():
            for c in cols:
                for b in ref:
                    b[:, c] = jnp.zeros((F, KC, CY), f32)

    clear(gx == 0, (u0, u1, q1, q2), (0, 1))
    clear(gx == nx - 1, (u0, u1, q1, q2), (CX + 2, CX + 3))

    @pl.when(gy == 0)
    def _():
        heard[:, 0] = jnp.zeros((4, 5, 8, CY), f32)

    @pl.when(gy == ny - 1)
    def _():
        heard[:, 1] = jnp.zeros((4, 5, 8, CY), f32)

    here(rw_in, rw, L_RW).wait()
    width = jnp.full((8, CY), rw[0], jnp.int32)
    scale = (width + 1).astype(f32)
    pos_y = gy * CY + lane
    wy = jnp.maximum(width - jnp.minimum(pos_y, ny * CY - 1 - pos_y), 0).astype(f32) / scale

    def wx_of(x):
        pos = gx * CX + x
        return jnp.maximum(width - jnp.minimum(pos, nx * CX - 1 - pos), 0).astype(f32) / scale

    def weights(x, c):
        ztab[x] = (1.0 - wx_of(x)) * (1.0 - wy)
        return c

    lax.fori_loop(0, CX, weights, 0)

    def rows(g):
        return pl.ds(8 * g, 8)

    def slot(x, f, g):
        if f < 4:
            return g, f // 2, 8 * x + 4 * (f % 2) + 2 * (f // 2)
        return 4, g // 2, 8 * x + 4 * (g % 2) + 2 * (g // 2)

    def put(acc, v, x, f, g):
        i, fam, p = slot(x, f, g)
        moved = pltpu.roll(jnp.where(ends2, v, 0.0), lax.rem(p + 2, CY), 1)
        acc[2 * i + fam] = acc[2 * i + fam] + moved

    def ship_y(r, acc):
        for i in range(10):
            own[r, i] = acc[i]
        for i in range(5):
            packs[r, 1, i] = jnp.where(quad, acc[2 * i], acc[2 * i + 1])
            packs[r, 0, i] = jnp.where(quad, acc[2 * i + 1], acc[2 * i])

        @pl.when(gy > 0)
        def _():
            send(packs.at[r, 0], heard.at[r, 1], 4 * r + DOWN, 4 * r + DOWN, {"gy": gy - 1}).start()

        @pl.when(gy < ny - 1)
        def _():
            send(packs.at[r, 1], heard.at[r, 0], 4 * r + UP, 4 * r + UP, {"gy": gy + 1}).start()

    def ship_x(r, ref):
        @pl.when(gx > 0)
        def _():
            send(ref.at[:, 2:4], ref.at[:, CX + 2 : CX + 4], 4 * r + LEFT, 4 * r + LEFT, {"gx": gx - 1}).start()

        @pl.when(gx < nx - 1)
        def _():
            send(ref.at[:, CX : CX + 2], ref.at[:, 0:2], 4 * r + RIGHT, 4 * r + RIGHT, {"gx": gx + 1}).start()

    def await_x(r, ref):
        @pl.when(gx > 0)
        def _():
            whole(ref.at[:, 0:2], rcv, 4 * r + RIGHT).wait()

        @pl.when(gx < nx - 1)
        def _():
            whole(ref.at[:, CX + 2 : CX + 4], rcv, 4 * r + LEFT).wait()

    def await_y(r):
        @pl.when(gy > 0)
        def _():
            whole(heard.at[r, 0], rcv, 4 * r + UP).wait()

        @pl.when(gy < ny - 1)
        def _():
            whole(heard.at[r, 1], rcv, 4 * r + DOWN).wait()

        for i in range(5):
            lo, hi = heard[r, 0, i], heard[r, 1, i]
            for fam in range(2):
                d = (jnp.where(quad, hi, lo) if fam else jnp.where(quad, lo, hi)) - own[r, 2 * i + fam]
                place = lax.rem(lane + 2 * fam, 4)
                near = jnp.where(place == 1, pltpu.roll(d, CY - 1, 1), jnp.where(place == 2, pltpu.roll(d, 1, 1), 0.0))
                far = jnp.where(place < 2, pltpu.roll(d, CY - 2, 1), pltpu.roll(d, 2, 1))
                halo[2 * i + fam] = near - 0.0625 * far

    def lap(ref, x, f, g):
        i, fam, p = slot(x, f, g)
        mend = jnp.where(ends2, pltpu.roll(halo[2 * i + fam], (CY - 2) - p, 1), 0.0)
        c = ref[f, x + 2, rows(g)]
        s1 = pltpu.roll(c, 1, 1) + pltpu.roll(c, CY - 1, 1)
        s2 = pltpu.roll(c, 2, 1) + pltpu.roll(c, CY - 2, 1)
        s1 = s1 + (ref[f, x + 1, rows(g)] + ref[f, x + 3, rows(g)])
        s2 = s2 + (ref[f, x, rows(g)] + ref[f, x + 4, rows(g)])
        return (s1 + mend) - 0.0625 * s2 - 3.75 * c, c

    none = tuple(zero for _ in range(10))

    here(mix_in, mix, L_MIX).wait()
    whole(dp, loc, L_DIF).wait()
    whole(a0, loc, L_COT).wait()

    def first(x, acc):
        acc = list(acc)
        z = ztab[x]
        for g in range(G):
            d = dp[x, rows(g)] * (4.0 / 3.0)
            dp[x, rows(g)] = d
            w = d * z
            dz[x, rows(g)] = w
            for f in range(F):
                v = w * a0[f, x, rows(g)]
                q1[f, x + 2, rows(g)] = v
                put(acc, v, x, f, g)
        return tuple(acc)

    ship = lax.fori_loop(0, CX, first, none)
    ship_x(R_Q1, q1)
    ship_y(R_Q1, ship)

    whole(u0.at[:, 2 : CX + 2], loc, L_STATE).wait()

    def second(x, acc):
        acc = list(acc)
        for g in range(G):
            for f in range(F):
                put(acc, u0[f, x + 2, rows(g)], x, f, g)
        return tuple(acc)

    ship_y(R_U0, lax.fori_loop(0, CX, second, none))

    taps = [[mix[a, b] * 0.25 + (1.0 if a == b else 0.0) for b in range(F)] for a in range(F)]

    def blend(v, f, back):
        total = (taps[0][f] if back else taps[f][0]) * v[0]
        for g in range(1, F):
            total = total + (taps[g][f] if back else taps[f][g]) * v[g]
        return total

    def retreat(src, q, dst, nxt, x, acc):
        acc = list(acc)
        z = ztab[x]
        for g in range(G):
            p = [z * src[f, x, rows(g)] for f in range(F)]
            for f in range(F):
                t, _ = lap(q, x, f, g)
                m = t + blend(p, f, True)
                dst[f, x, rows(g)] = m
                if nxt is not None:
                    v = dz[x, rows(g)] * m
                    nxt[f, x + 2, rows(g)] = v
                    put(acc, v, x, f, g)
        return tuple(acc)

    def advance(u, dst, shift, pack, x, acc):
        acc = list(acc)
        z = ztab[x]
        for g in range(G):
            d = dp[x, rows(g)]
            both = [lap(u, x, f, g) for f in range(F)]
            c = [b[1] for b in both]
            for f in range(F):
                v = z * (d * both[f][0] + blend(c, f, False)) + edge[f, x, rows(g)]
                dst[f, x + shift, rows(g)] = v
                if pack:
                    put(acc, v, x, f, g)
        return tuple(acc)

    def sweep(r, ref, step):
        await_y(r)
        acc = lax.fori_loop(2, CX - 2, step, none)
        await_x(r, ref)
        return lax.fori_loop(0, 4, lambda i, a: step(i + (i // 2) * (CX - 4), a), acc)

    acc = sweep(R_Q1, q1, functools.partial(retreat, a0, q1, mid, q2))
    ship_x(R_Q2, q2)
    ship_y(R_Q2, acc)

    here(twe_in, twe, L_TWE).wait()
    here(tsn_in, tsn, L_TSN).wait()

    def climb(d, t, width_of):
        arr = jnp.concatenate([d, jnp.zeros((8, width_of), f32)], 0)
        for b in (1, 2, 4):
            arr = jnp.where((t & b)[0:1] != 0, pltpu.roll(arr, b, 0), arr)
        tiles = [arr[8 * j : 8 * j + 8] for j in range(5)]
        for b, size in ((8, 6), (16, 8), (32, 12), (64, 16)):
            on, gap = (t & b) != 0, b // 8
            blank = jnp.zeros((8, width_of), f32)
            take = lambda j: tiles[j] if 0 <= j < len(tiles) else blank
            tiles = [jnp.where(on, take(j - gap), take(j)) for j in range(size)]
        return tiles

    def descend(tiles, t):
        for b, size in ((64, 12), (32, 8), (16, 6), (8, 5)):
            on, gap = (t & b) != 0, b // 8
            tiles = [jnp.where(on, tiles[j + gap], tiles[j]) if j + gap < len(tiles) else tiles[j] for j in range(size)]
        arr = jnp.concatenate(tiles, 0)
        for b in (4, 2, 1):
            arr = jnp.where((t & b)[0:1] != 0, pltpu.roll(arr, 40 - b, 0), arr)
        return arr[0:KC]

    t_we = jnp.broadcast_to(jnp.where(gx == 0, twe[0:1], twe[1:2]), (8, CY))
    t_sn = jnp.broadcast_to(jnp.where(gy == 0, tsn[0:1], tsn[1:2]), (8, CX))

    @pl.when(x_end)
    def _():
        def one(f, c):
            def add(x, s):
                return s + jnp.tile((1.0 - wy) * wx_of(x), (G, 1)) * (a0[f, x] + mid[f, x])

            tiles = climb(lax.fori_loop(0, CX, add, jnp.zeros((KC, CY), f32)), t_we, CY)
            for j in range(16):
                gw[2 * j, f] = tiles[j][0:4]
                gw[2 * j + 1, f] = tiles[j][4:8]
            return c

        lax.fori_loop(0, F, one, 0)

    @pl.when(y_end)
    def _():
        def one(f, c):
            col = lax.broadcasted_iota(jnp.int32, (KC, CX), 1)

            def add(x, s):
                v = jnp.sum(jnp.tile(wy, (G, 1)) * (a0[f, x] + mid[f, x]), axis=1, keepdims=True)
                return jnp.where(col == x, v, s)

            tiles = climb(lax.fori_loop(0, CX, add, jnp.zeros((KC, CX), f32)), t_sn, CX)
            for j in range(16):
                gs[j // 2, f, 8 * (j % 2) : 8 * (j % 2) + 8] = tiles[j]
            return c

        lax.fori_loop(0, F, one, 0)

    spread = (("gx", gx, nx, gw, gwe, S_GWE, L_GWE), ("gy", gy, ny, gs, gsn, S_GSN, L_GSN))
    for axis, at, n, src, dst, s, l in spread:
        for e, end in ((0, 0), (1, n - 1)):
            @pl.when(at == end)
            def _():
                here(src.at[end], dst.at[e], l).start()

                def one(i, c):
                    to = i + 1 if e == 0 else i
                    send(src.at[to], dst.at[e], s, s + e, {axis: to}).start()
                    return c

                lax.fori_loop(0, n - 1, one, 0)

    for axis, at, n, src, dst, s, l in gather:
        for e, end in ((0, 0), (1, n - 1)):
            @pl.when(at == end)
            def _():
                rest = dst.at[1:n] if e == 0 else dst.at[0 : n - 1]
                whole(rest, rcv, s).wait()
                here(src.at[e], dst.at[end], l).wait()

    @pl.when(x_end)
    def _():
        def one(f, c):
            tiles = [jnp.concatenate([pwe[2 * j, f], pwe[2 * j + 1, f]], 0) for j in range(16)]
            bwe[f] = descend(tiles, t_we)
            return c

        lax.fori_loop(0, F, one, 0)

    @pl.when(jnp.logical_not(x_end))
    def _():
        bwe[...] = jnp.zeros((F, KC, CY), f32)

    @pl.when(y_end)
    def _():
        def one(f, c):
            tiles = [psn[j // 2, f, 8 * (j % 2) : 8 * (j % 2) + 8] for j in range(16)]
            bsn[f] = descend(tiles, t_sn)
            return c

        lax.fori_loop(0, F, one, 0)

    @pl.when(jnp.logical_not(y_end))
    def _():
        bsn[...] = jnp.zeros((F, KC, CX), f32)

    @pl.when(x_end | y_end)
    def _():
        def one(f, c):
            b = bsn[f]
            for x in range(CX):
                w = jnp.tile((1.0 - wy) * wx_of(x), (G, 1))
                edge[f, x] = w * bwe[f] + jnp.tile(wy, (G, 1)) * b[:, x : x + 1]
            return c

        lax.fori_loop(0, F, one, 0)

    @pl.when(jnp.logical_not(x_end | y_end))
    def _():
        def one(x, c):
            edge[:, x] = jnp.zeros((F, KC, CY), f32)
            return c

        lax.fori_loop(0, CX, one, 0)

    acc = sweep(R_U0, u0, functools.partial(advance, u0, u1, 2, True))
    ship_x(R_U1, u1)
    ship_y(R_U1, acc)

    sweep(R_Q2, q2, functools.partial(retreat, mid, q2, out_g, None))
    for x in range(CX):
        here(out_g.at[:, x], grad.at[:, :, x, :], L_GRAD).start()

    sweep(R_U1, u1, functools.partial(advance, u1, out_f, 0, False))
    for x in range(CX):
        here(out_f.at[:, x], final.at[:, :, x, :], L_FINAL).start()

    for r, ref in ((R_Q1, q1), (R_U0, u0), (R_Q2, q2), (R_U1, u1)):
        pair = ref.at[:, 0:2]
        for way, cond, what in (
            (LEFT, gx > 0, pair), (RIGHT, gx < nx - 1, pair),
            (DOWN, gy > 0, packs.at[r, 0]), (UP, gy < ny - 1, packs.at[r, 1]),
        ):
            @pl.when(cond)
            def _():
                whole(what, snd, 4 * r + way).wait()

    for axis, at, n, src, dst, s, l in gather:
        for e, end in ((0, 0), (1, n - 1)):
            @pl.when(at != end)
            def _():
                whole(src.at[e], snd, s + e).wait()

    for axis, at, n, src, dst, s, l in spread:
        for e, end in ((0, 0), (1, n - 1)):
            @pl.when(at == end)
            def _():
                whole(src.at[1:n] if e == 0 else src.at[0 : n - 1], snd, s).wait()
                here(src.at[end], dst.at[e], l).wait()

            @pl.when(at != end)
            def _():
                whole(dst.at[e], rcv, s + e).wait()

    whole(out_g, loc, L_GRAD).wait()
    whole(out_f, loc, L_FINAL).wait()


def solution(mesh):
    nx, ny = mesh.shape["gx"], mesh.shape["gy"]
    wide, flat = (F, CX + 4, KC, CY), (F, CX, KC, CY)

    def body(*args):
        anywhere = pl.BlockSpec(memory_space=pl.ANY)
        scratch = [wide] * 4 + [flat] * 5 + [
            (CX, KC, CY), (CX, KC, CY), (CX, 8, CY),
            (nx, F, KP // nx, CY), (ny, F, KP // ny, CX), (F, KC, CY), (F, KC, CX),
            (nx, F, KP // nx, CY), (ny, F, KP // ny, CX),
            (4, 2, 5, 8, CY), (4, 2, 5, 8, CY), (4, 10, 8, CY), (10, 8, CY),
        ]
        child = jax.ShapeDtypeStruct((F, KC, CX, CY), f32)
        return pl.pallas_call(
            functools.partial(kernel, nx, ny),
            out_shape=(
                child, child,
                jax.ShapeDtypeStruct((2, F, KP // nx, CY), f32),
                jax.ShapeDtypeStruct((2, F, KP // ny, CX), f32),
            ),
            in_specs=[anywhere] * 9,
            out_specs=[anywhere] * 4,
            scratch_shapes=[pltpu.VMEM(s, f32) for s in scratch] + [
                pltpu.VMEM((2, CY), jnp.int32),
                pltpu.VMEM((2, CX), jnp.int32),
                pltpu.SMEM((F, F), f32),
                pltpu.SMEM((1,), jnp.int32),
                pltpu.SemaphoreType.DMA((13,)),
                pltpu.SemaphoreType.DMA((NSEM,)),
                pltpu.SemaphoreType.DMA((NSEM,)),
            ],
            compiler_params=pltpu.CompilerParams(
                collective_id=0, has_side_effects=True, vmem_limit_bytes=56 * 2**20
            ),
            name="nest",
        )(*args)

    return jax.shard_map(
        body,
        mesh=mesh,
        in_specs=(
            P(None, None, "gx", "gy"),
            P(None, None, "gx", "gy"),
            P(None, "gx", "gy"),
            P(),
            P(None, None, "gx", "gy"),
            P(None, None, "gy", "gx"),
            P(None, "gy"),
            P(None, "gx"),
            P(),
        ),
        out_specs=(
            P(None, None, "gx", "gy"),
            P(None, None, "gx", "gy"),
            P(None, None, "gx", "gy"),
            P(None, None, "gy", "gx"),
        ),
        check_vma=False,
    )
```

```python
import functools

import jax
import jax.numpy as jnp
from jax import lax
from jax.experimental import pallas as pl
from jax.experimental.pallas import tpu as pltpu
from jax.sharding import PartitionSpec as P

MESH = pl.DeviceIdType.MESH
F, KC, KP, CX, CY = 5, 32, 128, 16, 128
G = KC // 8
f32 = jnp.float32

L_COT, L_DIF, L_STATE, L_TWE, L_TSN, L_PWE, L_PSN, L_GWE, L_GSN, L_MIX, L_RW, L_GRAD, L_FINAL = range(13)
R_Q1, R_U0, R_Q2, R_U1 = range(4)
LEFT, RIGHT, DOWN, UP = range(4)
S_PWE, S_PSN, S_GWE, S_GSN = 16, 18, 20, 22
S_PWE2, S_GWE2 = 24, 25
NSEM = 26
VMEM_LIMIT = 56 * 2**20
W = 8


def tile(shape_dim):
    return lax.broadcasted_iota(jnp.int32, (8, CY), shape_dim)


def kernel(
    nx, ny,
    state, cot, dif, mix_in, pwe_in, psn_in, twe_in, tsn_in, rw_in,
    final, grad, gwe, gsn,
    u0, u1, q1, q2, a0, mid, out_f, out_g, edge, dp, dz, ztab, xtab,
    pwe, psn, bwe, bsn, gw, gs, packs, heard, own, halo, twe, tsn, mix, rw,
    loc, snd, rcv, above, opened, entered,
):
    gx, gy = lax.axis_index("gx"), lax.axis_index("gy")
    lane = tile(1)
    low2, high2, quad = lane < 2, lane >= CY - 2, lax.rem(lane, 4) < 2
    ends2 = low2 | high2
    x_end, y_end = (gx == 0) | (gx == nx - 1), (gy == 0) | (gy == ny - 1)

    def here(src, dst, sem):
        return pltpu.make_async_copy(src, dst, loc.at[sem])

    def whole(ref, sems, i):
        return pltpu.make_async_copy(ref, ref, sems.at[i])

    barrier = pltpu.get_barrier_semaphore()

    def greet(cond, to):
        @pl.when(cond)
        def _():
            pl.semaphore_signal(barrier, inc=1, device_id=to, device_id_type=MESH)

    base = gx // W * W
    subs = (base, base + W - 1)
    west, east = gx == subs[0], gx == subs[1]
    both = [(gx > 0, {"gx": gx - 1}), (gx < nx - 1, {"gx": gx + 1})]
    for e, sub in enumerate(subs):
        both.append((gx != sub, {"gx": sub}))
        for j in range(W - 1):
            both.append((gx == sub, {"gx": base + j + 1 - e}))
    told = [(gy < ny - 1, {"gy": gy + 1}), (gy < ny - 1, {"gy": jnp.int32(ny - 1)})]
    told += [(gy == 0, {"gy": jnp.int32(j)}) for j in range(1, ny)]
    told += [(gx == 0, {"gx": jnp.int32(j)}) for j in range(W, nx, W)]
    told += [(east & (gx < nx - 1), {"gx": jnp.int32(nx - 1)})]
    for cond, to in both + told:
        greet(cond, to)
    wanted = sum(cond.astype(jnp.int32) for cond, _ in both)
    wanted = wanted + jnp.where(gy > 0, 2, 0) + jnp.where(gy == ny - 1, ny - 1, 0)
    wanted = wanted + jnp.where(west & (gx > 0), 1, 0) + jnp.where(gx == nx - 1, nx // W - 1, 0)

    here(rw_in, rw, L_RW).start()
    for x in range(CX):
        here(cot.at[:, :, x, :], a0.at[:, x], L_COT).start()
        here(dif.at[:, x, :], dp.at[x], L_DIF).start()
    here(mix_in, mix, L_MIX).start()
    for x in range(CX):
        here(state.at[:, :, x, :], u0.at[:, x + 2], L_STATE).start()
    here(twe_in, twe, L_TWE).start()
    here(tsn_in, tsn, L_TSN).start()

    def send(src, dst, i, j, to):
        return pltpu.make_async_remote_copy(src_ref=src, dst_ref=dst, send_sem=snd.at[i], recv_sem=rcv.at[j], device_id=to, device_id_type=MESH)

    def clear(cond, ref, cols):
        @pl.when(cond)
        def _():
            for c in cols:
                for b in ref:
                    b[:, c] = jnp.zeros((F, KC, CY), f32)

    clear(gx == 0, (u0, u1, q1, q2), (0, 1))
    clear(gx == nx - 1, (u0, u1, q1, q2), (CX + 2, CX + 3))

    @pl.when(gy == 0)
    def _():
        heard[:, 0] = jnp.zeros((4, 5, 8, CY), f32)

    @pl.when(gy == ny - 1)
    def _():
        heard[:, 1] = jnp.zeros((4, 5, 8, CY), f32)

    here(rw_in, rw, L_RW).wait()
    width = jnp.broadcast_to(rw[...], (8, CY))
    scale = (width + 1).astype(f32)
    pos_y = gy * CY + lane
    wy = jnp.maximum(width - jnp.minimum(pos_y, ny * CY - 1 - pos_y), 0).astype(f32) / scale

    def wx_of(x):
        pos = gx * CX + x
        return jnp.maximum(width - jnp.minimum(pos, nx * CX - 1 - pos), 0).astype(f32) / scale

    def weights(x, c):
        wx = wx_of(x)
        ztab[x] = (1.0 - wx) * (1.0 - wy)
        xtab[x] = (1.0 - wy) * wx
        return c

    lax.fori_loop(0, CX, weights, 0)

    def rows(g):
        return pl.ds(pl.multiple_of(8 * g, 8), 8)

    def slot(x, f):
        return (0, 8 * x + 4 * f) if f < 2 else (1, 8 * x + 4 * (f - 2) + 2) if f < 4 else (2, 8 * x)

    def put(acc, v, x, f):
        i, p = slot(x, f)
        acc[i] = acc[i] + pltpu.roll(jnp.where(ends2, v, 0.0), (p + 2) % CY, 1)

    def own_of(r, i):
        if i < G:
            return own[r, i, 0], own[r, i, 1]
        return own[r, 0, 2] + pltpu.roll(own[r, 1, 2], 4, 1), pltpu.roll(own[r, 2, 2], 2, 1) + pltpu.roll(own[r, 3, 2], 6, 1)

    def ship_y(r):
        for i in range(5):
            one, two = own_of(r, i)
            packs[r, 1, i] = jnp.where(quad, one, two)
            packs[r, 0, i] = jnp.where(quad, two, one)

        @pl.when(gy > 0)
        def _():
            send(packs.at[r, 0], heard.at[r, 1], 4 * r + DOWN, 4 * r + DOWN, {"gy": gy - 1}).start()

        if r in (R_Q2, R_U1):
            ship_up(r, gy < ny - 1)

    def ship_up(r, cond):
        @pl.when(cond)
        def _():
            if r == R_Q1:
                pl.semaphore_wait(above, 1)
            send(packs.at[r, 1], heard.at[r, 0], 4 * r + UP, 4 * r + UP, {"gy": gy + 1}).start()

    def ship_x(r, ref):
        @pl.when(gx > 0)
        def _():
            send(ref.at[:, 2:4], ref.at[:, CX + 2 : CX + 4], 4 * r + LEFT, 4 * r + LEFT, {"gx": gx - 1}).start()

        @pl.when(gx < nx - 1)
        def _():
            send(ref.at[:, CX : CX + 2], ref.at[:, 0:2], 4 * r + RIGHT, 4 * r + RIGHT, {"gx": gx + 1}).start()

    def await_x(r, ref):
        @pl.when(gx > 0)
        def _():
            whole(ref.at[:, 0:2], rcv, 4 * r + RIGHT).wait()

        @pl.when(gx < nx - 1)
        def _():
            whole(ref.at[:, CX + 2 : CX + 4], rcv, 4 * r + LEFT).wait()

    def await_y(r):
        @pl.when(gy > 0)
        def _():
            whole(heard.at[r, 0], rcv, 4 * r + UP).wait()

        @pl.when(gy < ny - 1)
        def _():
            whole(heard.at[r, 1], rcv, 4 * r + DOWN).wait()

        for i in range(5):
            lo, hi = heard[r, 0, i], heard[r, 1, i]
            mends = []
            for fam, mine in enumerate(own_of(r, i)):
                d = (jnp.where(quad, hi, lo) if fam else jnp.where(quad, lo, hi)) - mine
                place = lax.rem(lane + 2 * fam, 4)
                near = jnp.where(place == 1, pltpu.roll(d, CY - 1, 1), jnp.where(place == 2, pltpu.roll(d, 1, 1), 0.0))
                far = jnp.where(place < 2, pltpu.roll(d, CY - 2, 1), pltpu.roll(d, 2, 1))
                mends.append(near - 0.0625 * far)
            if i < G:
                halo[i, 0], halo[i, 1] = mends
            else:
                halo[0, 2] = mends[0]
                halo[1, 2] = pltpu.roll(mends[0], CY - 4, 1)
                halo[2, 2] = pltpu.roll(mends[1], CY - 2, 1)
                halo[3, 2] = pltpu.roll(mends[1], CY - 6, 1)

    def mend(x, f, g):
        i, p = slot(x, f)
        return jnp.where(ends2, pltpu.roll(halo[g, i], (CY - 2) - p, 1), 0.0)

    def lap(ref, x, f, g):
        c = ref[f, x + 2, rows(g)]
        s1 = pltpu.roll(c, 1, 1) + pltpu.roll(c, CY - 1, 1)
        s2 = pltpu.roll(c, 2, 1) + pltpu.roll(c, CY - 2, 1)
        s1 = s1 + (ref[f, x + 1, rows(g)] + ref[f, x + 3, rows(g)])
        s2 = s2 + (ref[f, x, rows(g)] + ref[f, x + 4, rows(g)])
        return s1 - 0.0625 * s2 - 3.75 * c, c

    def per_group(cols, step):
        def one(g, c):
            for x in cols:
                step(x, g)
            return c

        lax.fori_loop(0, G, one, 0)

    def pack(r, value):
        def one(g, c):
            acc = [jnp.zeros((8, CY), f32) for _ in range(3)]
            for x in range(CX):
                for f in range(F):
                    put(acc, value(x, f, g), x, f)
            for i in range(3):
                own[r, g, i] = acc[i]
            return c

        lax.fori_loop(0, G, one, 0)

    pl.semaphore_wait(barrier, wanted)
    @pl.when(gx > 0)
    def _():
        for i in range(2):
            send(state.at[:, :, i, :], u0.at[:, CX + 2 + i], 4 * R_U0 + LEFT, 4 * R_U0 + LEFT, {"gx": gx - 1}).start()

    @pl.when(gx < nx - 1)
    def _():
        for i in range(2):
            send(state.at[:, :, CX - 2 + i, :], u0.at[:, i], 4 * R_U0 + RIGHT, 4 * R_U0 + RIGHT, {"gx": gx + 1}).start()

    def signal(sem, axis, to):
        pl.semaphore_signal(sem, inc=1, device_id={axis: jnp.int32(to)}, device_id_type=MESH)

    @pl.when(gy > 0)
    def _():
        signal(above, "gy", gy - 1)
        signal(entered.at[1], "gy", 0)
        send(psn_in.at[0], psn.at[gy], S_PSN, S_PSN, {"gy": jnp.int32(0)}).start()

    @pl.when(gy == ny - 1)
    def _():
        for i in range(ny - 1):
            signal(opened.at[1], "gy", i)

    @pl.when(west & (gx > 0))
    def _():
        signal(entered.at[0], "gx", 0)

    @pl.when(gx == nx - 1)
    def _():
        for i in range(W - 1, nx - 1, W):
            signal(opened.at[0], "gx", i)

    whole(dp, loc, L_DIF).wait()
    whole(a0, loc, L_COT).wait()

    def first(x, g):
        d = dp[x, rows(g)] * (4.0 / 3.0)
        dp[x, rows(g)] = d
        w = d * ztab[x]
        dz[x, rows(g)] = w
        for f in range(F):
            v = w * a0[f, x, rows(g)]
            q1[f, x + 2, rows(g)] = v

    per_group(range(CX), first)
    pack(R_Q1, lambda x, f, g: q1[f, x + 2, rows(g)])

    ship_x(R_Q1, q1)
    ship_y(R_Q1)
    for e, sub in enumerate(subs):
        @pl.when(gx != sub)
        def _():
            send(pwe_in.at[e], pwe.at[gx], S_PWE + e, S_PWE, {"gx": sub}).start()

        @pl.when(gx == sub)
        def _():
            here(pwe_in.at[e], pwe.at[gx], L_PWE).start()

        @pl.when(gy == e * (ny - 1))
        def _():
            here(psn_in.at[e], psn.at[gy], L_PSN).start()

    whole(u0.at[:, 2 : CX + 2], loc, L_STATE).wait()

    pack(R_U0, lambda x, f, g: u0[f, x + 2, rows(g)])
    ship_y(R_U0)

    here(mix_in, mix, L_MIX).wait()
    taps = [[mix[a, b] * 0.25 + (1.0 if a == b else 0.0) for b in range(F)] for a in range(F)]

    def blend(v, f, back):
        total = (taps[0][f] if back else taps[f][0]) * v[0]
        for g in range(1, F):
            total = total + (taps[g][f] if back else taps[f][g]) * v[g]
        return total

    def retreat(src, q, dst, x, g):
        z = ztab[x]
        p = [z * src[f, x, rows(g)] for f in range(F)]
        for f in range(F):
            t, _ = lap(q, x, f, g)
            dst[f, x, rows(g)] = t + blend(p, f, True)

    def advance(u, dst, shift, x, g):
        z, d = ztab[x], dp[x, rows(g)]
        both = [lap(u, x, f, g) for f in range(F)]
        c = [b[1] for b in both]
        for f in range(F):
            dst[f, x + shift, rows(g)] = z * (d * both[f][0] + blend(c, f, False))

    def sweep(r, ref, step, between=None):
        per_group(range(2, CX - 2), step)
        if between is not None:
            between()
        await_x(r, ref)
        per_group((0, 1, CX - 2, CX - 1), step)

    def block_to(root):
        block = pwe.at[pl.ds(base, W)]
        return send(block, block, S_PWE2, S_PWE2, {"gx": jnp.int32(root)})

    def take_columns():
        for e, sub in enumerate(subs):
            @pl.when(gx == sub)
            def _():
                whole(pwe.at[pl.ds(base + 1 - e, W - 1)], rcv, S_PWE).wait()
                here(pwe_in.at[e], pwe.at[gx], L_PWE).wait()

        @pl.when(west & (gx > 0))
        def _():
            block_to(0).start()

        @pl.when(east & (gx < nx - 1))
        def _():
            pl.semaphore_wait(opened.at[0], 1)
            block_to(nx - 1).start()

    sweep(R_U0, u0, functools.partial(advance, u0, u1, 2))

    middle = gy == ny // 2 - 1
    ship_up(R_Q1, (gy < ny - 1) & jnp.logical_not(middle))
    ship_up(R_U0, (gy < ny - 1) & jnp.logical_not(middle))

    sweep(R_Q1, q1, functools.partial(retreat, a0, q1, mid), take_columns)

    ship_up(R_Q1, middle)
    ship_up(R_U0, middle)
    await_y(R_Q1)

    def settle_middle(x, f, g):
        m = mid[f, x, rows(g)] + mend(x, f, g)
        mid[f, x, rows(g)] = m
        v = dz[x, rows(g)] * m
        q2[f, x + 2, rows(g)] = v
        return v

    pack(R_Q2, settle_middle)
    ship_x(R_Q2, q2)
    ship_y(R_Q2)
    here(twe_in, twe, L_TWE).wait()
    here(tsn_in, tsn, L_TSN).wait()

    def climb(d, t, width_of):
        arr = jnp.concatenate([d, jnp.zeros((8, width_of), f32)], 0)
        for b in (1, 2, 4):
            arr = jnp.where((t & b)[0:1] != 0, pltpu.roll(arr, b, 0), arr)
        tiles = [arr[8 * j : 8 * j + 8] for j in range(5)]
        for b, size in ((8, 6), (16, 8), (32, 12), (64, 16)):
            on, gap = (t & b) != 0, b // 8
            blank = jnp.zeros((8, width_of), f32)
            take = lambda j: tiles[j] if 0 <= j < len(tiles) else blank
            tiles = [jnp.where(on, take(j - gap), take(j)) for j in range(size)]
        return tiles

    def descend(tiles, t):
        for b, size in ((64, 12), (32, 8), (16, 6), (8, 5)):
            on, gap = (t & b) != 0, b // 8
            tiles = [jnp.where(on, tiles[j + gap], tiles[j]) if j + gap < len(tiles) else tiles[j] for j in range(size)]
        arr = jnp.concatenate(tiles, 0)
        for b in (4, 2, 1):
            arr = jnp.where((t & b)[0:1] != 0, pltpu.roll(arr, 40 - b, 0), arr)
        return arr[0:KC]

    t_we = jnp.broadcast_to(jnp.where(gx == 0, twe[0:1], twe[1:2]), (8, CY))
    t_sn = jnp.broadcast_to(jnp.where(gy == 0, tsn[0:1], tsn[1:2]), (8, CX))

    @pl.when(x_end)
    def _():
        def one(f, c):
            d = []
            for g in range(G):
                s = xtab[0] * (a0[f, 0, rows(g)] + mid[f, 0, rows(g)])
                for x in range(1, CX):
                    s = s + xtab[x] * (a0[f, x, rows(g)] + mid[f, x, rows(g)])
                d.append(s)
            tiles = climb(jnp.concatenate(d, 0), t_we, CY)
            for j in range(16):
                gw[2 * j, f] = tiles[j][0:4]
                gw[2 * j + 1, f] = tiles[j][4:8]
            return c

        lax.fori_loop(0, F, one, 0)

    @pl.when(y_end)
    def _():
        def one(f, c):
            col = lax.broadcasted_iota(jnp.int32, (8, CX), 1)
            d = []
            for g in range(G):
                s = jnp.zeros((8, CX), f32)
                for x in range(CX):
                    v = jnp.sum(wy * (a0[f, x, rows(g)] + mid[f, x, rows(g)]), axis=1, keepdims=True)
                    s = jnp.where(col == x, v, s)
                d.append(s)
            tiles = climb(jnp.concatenate(d, 0), t_sn, CX)
            for j in range(16):
                gs[j // 2, f, 8 * (j % 2) : 8 * (j % 2) + 8] = tiles[j]
            return c

        lax.fori_loop(0, F, one, 0)

    def spread_we(e):
        root = e * (nx - 1)
        for j in range(nx // W):
            if j != root // W:
                block = gw.at[pl.ds(j * W, W)]
                send(block, block, S_GWE2, S_GWE2, {"gx": jnp.int32(j * W + e * (W - 1))}).start()

    def spread_sn(e):
        root = e * (ny - 1)
        here(gs.at[root], gsn.at[e], L_GSN).start()
        for j in range(ny):
            if j != root:
                send(gs.at[j], gsn.at[e], S_GSN, S_GSN + e, {"gy": jnp.int32(j)}).start()

    for e in range(2):
        @pl.when(gx == e * (nx - 1))
        def _():
            if e == 0:
                pl.semaphore_wait(entered.at[0], nx // W - 1)
            spread_we(e)

        @pl.when(gy == e * (ny - 1))
        def _():
            if e == 0:
                pl.semaphore_wait(entered.at[1], ny - 1)
            spread_sn(e)

    def relay_gradients():
        for e, sub in enumerate(subs):
            @pl.when((gx == sub) & (gx != e * (nx - 1)))
            def _():
                whole(gw.at[pl.ds(base, W)], rcv, S_GWE2).wait()

            @pl.when(gx == sub)
            def _():
                here(gw.at[gx], gwe.at[e], L_GWE).start()
                for j in range(W - 1):
                    to = base + j + 1 - e
                    send(gw.at[to], gwe.at[e], S_GWE, S_GWE + e, {"gx": to}).start()
    @pl.when(gy < ny - 1)
    def _():
        pl.semaphore_wait(opened.at[1], 1)
        send(psn_in.at[1], psn.at[gy], S_PSN + 1, S_PSN + 1, {"gy": jnp.int32(ny - 1)}).start()

    for e in range(2):
        @pl.when(gx == e * (nx - 1))
        def _():
            whole(pwe.at[0 : nx - W] if e else pwe.at[W:nx], rcv, S_PWE2).wait()

        @pl.when(gy == e * (ny - 1))
        def _():
            whole(psn.at[0 : ny - 1] if e else psn.at[1:ny], rcv, S_PSN + e).wait()
            here(psn_in.at[e], psn.at[gy], L_PSN).wait()

    @pl.when(x_end)
    def _():
        def one(f, c):
            tiles = [jnp.concatenate([pwe[2 * j, f], pwe[2 * j + 1, f]], 0) for j in range(16)]
            bwe[f] = descend(tiles, t_we)
            return c

        lax.fori_loop(0, F, one, 0)

    @pl.when(y_end & jnp.logical_not(x_end))
    def _():
        bwe[...] = jnp.zeros((F, KC, CY), f32)

    @pl.when(y_end)
    def _():
        def one(f, c):
            tiles = [psn[j // 2, f, 8 * (j % 2) : 8 * (j % 2) + 8] for j in range(16)]
            bsn[f] = descend(tiles, t_sn)
            return c

        lax.fori_loop(0, F, one, 0)

    @pl.when(x_end & jnp.logical_not(y_end))
    def _():
        bsn[...] = jnp.zeros((F, KC, CX), f32)

    @pl.when(x_end | y_end)
    def _():
        def one(f, c):
            b = bsn[f]
            for x in range(CX):
                for g in range(G):
                    v = xtab[x] * bwe[f, rows(g)] + wy * b[8 * g : 8 * g + 8, x : x + 1]
                    edge[f, x, rows(g)] = v
                    u1[f, x + 2, rows(g)] = u1[f, x + 2, rows(g)] + v
            return c

        lax.fori_loop(0, F, one, 0)

    await_y(R_U0)

    def settle_first(x, f, g):
        v = u1[f, x + 2, rows(g)] + dz[x, rows(g)] * mend(x, f, g)
        u1[f, x + 2, rows(g)] = v
        return v

    pack(R_U1, settle_first)
    ship_x(R_U1, u1)
    ship_y(R_U1)

    sweep(R_Q2, q2, functools.partial(retreat, mid, q2, out_g))

    sweep(R_U1, u1, functools.partial(advance, u1, out_f, 0))

    relay_gradients()

    @pl.when(x_end | y_end)
    def _():
        def one(f, c):
            for x in range(CX):
                out_f[f, x] = out_f[f, x] + edge[f, x]
            return c

        lax.fori_loop(0, F, one, 0)

    await_y(R_Q2)

    def settle_grad(x, g):
        for f in range(F):
            out_g[f, x, rows(g)] = out_g[f, x, rows(g)] + mend(x, f, g)

    per_group(range(CX), settle_grad)
    for x in range(CX):
        here(out_g.at[:, x], grad.at[:, :, x, :], L_GRAD).start()
    await_y(R_U1)

    def settle_final(x, g):
        for f in range(F):
            out_f[f, x, rows(g)] = out_f[f, x, rows(g)] + dz[x, rows(g)] * mend(x, f, g)

    per_group(range(CX), settle_final)
    for x in range(CX):
        here(out_f.at[:, x], final.at[:, :, x, :], L_FINAL).start()

    for r, ref in ((R_Q1, q1), (R_U0, u0), (R_Q2, q2), (R_U1, u1)):
        pair = ref.at[:, 0:2]
        for way, cond, what in (
            (LEFT, gx > 0, pair), (RIGHT, gx < nx - 1, pair),
            (DOWN, gy > 0, packs.at[r, 0]), (UP, gy < ny - 1, packs.at[r, 1]),
        ):
            @pl.when(cond)
            def _():
                whole(what, snd, 4 * r + way).wait()

    for e, sub in enumerate(subs):
        root = e * (nx - 1)

        @pl.when(gx != sub)
        def _():
            whole(pwe_in.at[e], snd, S_PWE + e).wait()
            whole(gwe.at[e], rcv, S_GWE + e).wait()

        @pl.when(gx == sub)
        def _():
            whole(gw.at[pl.ds(base + 1 - e, W - 1)], snd, S_GWE).wait()
            here(gw.at[gx], gwe.at[e], L_GWE).wait()

        @pl.when((gx == sub) & (gx != root))
        def _():
            whole(pwe.at[pl.ds(base, W)], snd, S_PWE2).wait()

        @pl.when(gx == root)
        def _():
            whole(gw.at[0 : nx - W] if e else gw.at[W:nx], snd, S_GWE2).wait()

        last = e * (ny - 1)

        @pl.when(gy != last)
        def _():
            whole(psn_in.at[e], snd, S_PSN + e).wait()
            whole(gsn.at[e], rcv, S_GSN + e).wait()

        @pl.when(gy == last)
        def _():
            whole(gs.at[0 : ny - 1] if e else gs.at[1:ny], snd, S_GSN).wait()
            here(gs.at[last], gsn.at[e], L_GSN).wait()

    whole(out_g, loc, L_GRAD).wait()
    whole(out_f, loc, L_FINAL).wait()


def store(*refs):
    sources, targets, stage, sems = refs[:4], refs[4:8], refs[8:12], refs[12]
    moves = []
    for i, (src, mid, dst) in enumerate(zip(sources, stage, targets, strict=True)):
        for f in range(F if i < 2 else 1):
            a, b, c = (src.at[f], mid.at[f], dst.at[f]) if i < 2 else (src, mid, dst)
            moves.append((pltpu.make_async_copy(a, b, sems.at[0, i, f]), pltpu.make_async_copy(b, c, sems.at[1, i, f])))
    for first, _ in moves:
        first.start()
    for first, second in moves:
        first.wait()
        second.start()
    for _, second in moves:
        second.wait()


def solution(mesh):
    nx, ny = mesh.shape["gx"], mesh.shape["gy"]
    wide, flat = (F, CX + 4, KC, CY), (F, CX, KC, CY)

    def body(*args):
        far = pl.BlockSpec(memory_space=pltpu.HBM)
        scratch = [wide] * 4 + [flat] * 5 + [
            (CX, KC, CY), (CX, KC, CY), (CX, 8, CY), (CX, 8, CY),
            (nx, F, KP // nx, CY), (ny, F, KP // ny, CX), (F, KC, CY), (F, KC, CX),
            (nx, F, KP // nx, CY), (ny, F, KP // ny, CX),
            (4, 2, 5, 8, CY), (4, 2, 5, 8, CY), (4, G, 3, 8, CY), (G, 3, 8, CY),
        ]
        native = jax.ShapeDtypeStruct((F, KC, CX, CY), f32)
        edges = (
            jax.ShapeDtypeStruct((2, F, KP // nx, CY), f32),
            jax.ShapeDtypeStruct((2, F, KP // ny, CX), f32),
        )
        results = pl.pallas_call(
            functools.partial(kernel, nx, ny),
            out_shape=(native, native, *edges),
            in_specs=[far] * 9,
            out_specs=[far] * 4,
            scratch_shapes=[pltpu.VMEM(s, f32) for s in scratch] + [
                pltpu.VMEM((2, CY), jnp.int32),
                pltpu.VMEM((2, CX), jnp.int32),
                pltpu.SMEM((F, F), f32),
                pltpu.VMEM((1, 1), jnp.int32),
                pltpu.SemaphoreType.DMA((13,)),
                pltpu.SemaphoreType.DMA((NSEM,)),
                pltpu.SemaphoreType.DMA((NSEM,)),
                pltpu.SemaphoreType.REGULAR,
                pltpu.SemaphoreType.REGULAR((2,)),
                pltpu.SemaphoreType.REGULAR((2,)),
            ],
            compiler_params=pltpu.CompilerParams(
                collective_id=0, has_side_effects=True, vmem_limit_bytes=VMEM_LIMIT
            ),
            name="nest",
        )(*args[:8], args[8].reshape(1, 1))
        return pl.pallas_call(
            store,
            out_shape=(native, native, *edges),
            in_specs=[far] * 4,
            out_specs=[far] * 4,
            scratch_shapes=[pltpu.VMEM(o.shape, f32) for o in (native, native, *edges)] + [pltpu.SemaphoreType.DMA((2, 4, F))],
            compiler_params=pltpu.CompilerParams(vmem_limit_bytes=VMEM_LIMIT),
            name="store",
        )(*results)

    return jax.shard_map(
        body,
        mesh=mesh,
        in_specs=(
            P(None, None, "gx", "gy"),
            P(None, None, "gx", "gy"),
            P(None, "gx", "gy"),
            P(),
            P(None, None, "gx", "gy"),
            P(None, None, "gy", "gx"),
            P(None, "gy"),
            P(None, "gx"),
            P(),
        ),
        out_specs=(
            P(None, None, "gx", "gy"),
            P(None, None, "gx", "gy"),
            P(None, None, "gx", "gy"),
            P(None, None, "gy", "gx"),
        ),
        check_vma=False,
    )
```

```python
import functools

import jax
import jax.numpy as jnp
from jax import lax
from jax.experimental import pallas as pl
from jax.experimental.pallas import tpu as pltpu
from jax.sharding import PartitionSpec as P

MESH = pl.DeviceIdType.MESH
F, KC, KP, CX, CY = 5, 32, 128, 16, 128
G = KC // 8
INNER, OUTER = tuple(range(2, CX - 2)), (0, 1, CX - 2, CX - 1)
f32 = jnp.float32

L_COT, L_DIF, L_STATE, L_TWE, L_TSN, L_PWE, L_PSN, L_GWE, L_MIX, L_RW = range(10)
R_Q1, R_U0, R_Q2, R_U1 = range(4)
LEFT, RIGHT, DOWN, UP = range(4)
S_PWE, S_PSN, S_GWE, S_GSN = 16, 18, 20, 22
S_PWE2, S_GWE2 = 24, 25
NSEM = 26
VMEM_LIMIT = 40 * 2**20
W = 8


def tile(shape_dim):
    return lax.broadcasted_iota(jnp.int32, (8, CY), shape_dim)


def kernel(
    nx, ny,
    state, cot, dif, mix_in, pwe_in, psn_in, twe_in, tsn_in, rw_in,
    out_f, out_g, gwe, gsn,
    u0, u1, q1, q2, a0, mid, edge, dp, dz, ztab, xtab,
    pwe, psv, psd, psn, bwe, bsn, gw, gs, gsd, packs, heard, own, halo, twe, tsn, mix, rw,
    loc, snd, rcv, above, opened, entered,
):
    gx, gy = lax.axis_index("gx"), lax.axis_index("gy")
    lane = tile(1)
    low2, high2, quad = lane < 2, lane >= CY - 2, lax.rem(lane, 4) < 2
    ends2 = low2 | high2
    x_end, y_end = (gx == 0) | (gx == nx - 1), (gy == 0) | (gy == ny - 1)

    def here(src, dst, sem):
        return pltpu.make_async_copy(src, dst, loc.at[sem])

    def whole(ref, sems, i):
        return pltpu.make_async_copy(ref, ref, sems.at[i])

    barrier = pltpu.get_barrier_semaphore()

    def greet(cond, to):
        @pl.when(cond)
        def _():
            pl.semaphore_signal(barrier, inc=1, device_id=to, device_id_type=MESH)

    base = gx // W * W
    subs = (base, base + W - 1)
    west, east = gx == subs[0], gx == subs[1]
    both = [(gx > 0, {"gx": gx - 1}), (gx < nx - 1, {"gx": gx + 1})]
    for e, sub in enumerate(subs):
        both.append((gx != sub, {"gx": sub}))
        for j in range(W - 1):
            both.append((gx == sub, {"gx": base + j + 1 - e}))
    told = [(gy < ny - 1, {"gy": gy + 1}), (gy < ny - 1, {"gy": jnp.int32(ny - 1)})]
    told += [(gy == 0, {"gy": jnp.int32(j)}) for j in range(1, ny)]
    told += [(gx == 0, {"gx": jnp.int32(j)}) for j in range(W, nx, W)]
    told += [(east & (gx < nx - 1), {"gx": jnp.int32(nx - 1)})]
    for cond, to in both + told:
        greet(cond, to)
    wanted = sum(cond.astype(jnp.int32) for cond, _ in both)
    wanted = wanted + jnp.where(gy > 0, 2, 0) + jnp.where(gy == ny - 1, ny - 1, 0)
    wanted = wanted + jnp.where(west & (gx > 0), 1, 0) + jnp.where(gx == nx - 1, nx // W - 1, 0)

    here(rw_in, rw, L_RW).start()
    here(psn_in, psv, L_PSN).start()
    for x in range(CX):
        here(cot.at[:, :, x, :], a0.at[:, x], L_COT).start()
        here(dif.at[:, x, :], dp.at[x], L_DIF).start()
    here(mix_in, mix, L_MIX).start()
    for x in range(CX):
        here(state.at[:, :, x, :], u0.at[:, x + 2], L_STATE).start()
    here(twe_in, twe, L_TWE).start()
    here(tsn_in, tsn, L_TSN).start()

    def send(src, dst, i, j, to):
        return pltpu.make_async_remote_copy(src_ref=src, dst_ref=dst, send_sem=snd.at[i], recv_sem=rcv.at[j], device_id=to, device_id_type=MESH)

    def clear(cond, ref, cols):
        @pl.when(cond)
        def _():
            for c in cols:
                for b in ref:
                    b[:, c] = jnp.zeros((F, KC, CY), f32)

    clear(gx == 0, (u0, u1, q1, q2), (0, 1))
    clear(gx == nx - 1, (u0, u1, q1, q2), (CX + 2, CX + 3))

    @pl.when(gy == 0)
    def _():
        heard[:, 0] = jnp.zeros((4, 5, 8, CY), f32)

    @pl.when(gy == ny - 1)
    def _():
        heard[:, 1] = jnp.zeros((4, 5, 8, CY), f32)

    here(rw_in, rw, L_RW).wait()
    width = jnp.broadcast_to(rw[...], (8, CY))
    scale = (width + 1).astype(f32)
    pos_y = gy * CY + lane
    wy = jnp.maximum(width - jnp.minimum(pos_y, ny * CY - 1 - pos_y), 0).astype(f32) / scale

    def wx_of(x):
        pos = gx * CX + x
        return jnp.maximum(width - jnp.minimum(pos, nx * CX - 1 - pos), 0).astype(f32) / scale

    def weights(x, c):
        wx = wx_of(x)
        ztab[x] = (1.0 - wx) * (1.0 - wy)
        xtab[x] = (1.0 - wy) * wx
        return c

    lax.fori_loop(0, CX, weights, 0)

    def rows(g):
        return pl.ds(pl.multiple_of(8 * g, 8), 8)

    def slot(x, f):
        return (0, 8 * x + 4 * f) if f < 2 else (1, 8 * x + 4 * (f - 2) + 2) if f < 4 else (2, 8 * x)

    def put(acc, v, x, f):
        i, p = slot(x, f)
        acc[i] = acc[i] + pltpu.roll(jnp.where(ends2, v, 0.0), (p + 2) % CY, 1)

    def own_of(r, i):
        if i < G:
            return own[r, i, 0], own[r, i, 1]
        return own[r, 0, 2] + pltpu.roll(own[r, 1, 2], 4, 1), pltpu.roll(own[r, 2, 2], 2, 1) + pltpu.roll(own[r, 3, 2], 6, 1)

    def ship_y(r):
        for i in range(5):
            one, two = own_of(r, i)
            packs[r, 1, i] = jnp.where(quad, one, two)
            packs[r, 0, i] = jnp.where(quad, two, one)

        @pl.when(gy > 0)
        def _():
            send(packs.at[r, 0], heard.at[r, 1], 4 * r + DOWN, 4 * r + DOWN, {"gy": gy - 1}).start()

        if r in (R_Q2, R_U1):
            ship_up(r, gy < ny - 1)

    def ship_up(r, cond):
        @pl.when(cond)
        def _():
            if r == R_Q1:
                pl.semaphore_wait(above, 1)
            send(packs.at[r, 1], heard.at[r, 0], 4 * r + UP, 4 * r + UP, {"gy": gy + 1}).start()

    def ship_x(r, ref):
        @pl.when(gx > 0)
        def _():
            send(ref.at[:, 2:4], ref.at[:, CX + 2 : CX + 4], 4 * r + LEFT, 4 * r + LEFT, {"gx": gx - 1}).start()

        @pl.when(gx < nx - 1)
        def _():
            send(ref.at[:, CX : CX + 2], ref.at[:, 0:2], 4 * r + RIGHT, 4 * r + RIGHT, {"gx": gx + 1}).start()

    def await_x(r, ref):
        @pl.when(gx > 0)
        def _():
            whole(ref.at[:, 0:2], rcv, 4 * r + RIGHT).wait()

        @pl.when(gx < nx - 1)
        def _():
            whole(ref.at[:, CX + 2 : CX + 4], rcv, 4 * r + LEFT).wait()

    def await_y(r):
        @pl.when(gy > 0)
        def _():
            whole(heard.at[r, 0], rcv, 4 * r + UP).wait()

        @pl.when(gy < ny - 1)
        def _():
            whole(heard.at[r, 1], rcv, 4 * r + DOWN).wait()

        for i in range(5):
            lo, hi = heard[r, 0, i], heard[r, 1, i]
            mends = []
            for fam, mine in enumerate(own_of(r, i)):
                d = (jnp.where(quad, hi, lo) if fam else jnp.where(quad, lo, hi)) - mine
                place = lax.rem(lane + 2 * fam, 4)
                near = jnp.where(place == 1, pltpu.roll(d, CY - 1, 1), jnp.where(place == 2, pltpu.roll(d, 1, 1), 0.0))
                far = jnp.where(place < 2, pltpu.roll(d, CY - 2, 1), pltpu.roll(d, 2, 1))
                mends.append(near - 0.0625 * far)
            if i < G:
                halo[i, 0], halo[i, 1] = mends
            else:
                halo[0, 2] = mends[0]
                halo[1, 2] = pltpu.roll(mends[0], CY - 4, 1)
                halo[2, 2] = pltpu.roll(mends[1], CY - 2, 1)
                halo[3, 2] = pltpu.roll(mends[1], CY - 6, 1)

    def mend(x, f, g):
        i, p = slot(x, f)
        return jnp.where(ends2, pltpu.roll(halo[g, i], (CY - 2) - p, 1), 0.0)

    def lap(ref, x, f, g):
        c = ref[f, x + 2, rows(g)]
        s1 = pltpu.roll(c, 1, 1) + pltpu.roll(c, CY - 1, 1)
        s2 = pltpu.roll(c, 2, 1) + pltpu.roll(c, CY - 2, 1)
        s1 = s1 + (ref[f, x + 1, rows(g)] + ref[f, x + 3, rows(g)])
        s2 = s2 + (ref[f, x, rows(g)] + ref[f, x + 4, rows(g)])
        return s1 - 0.0625 * s2 - 3.75 * c, c

    def per_group(cols, step):
        def one(g, c):
            for x in cols:
                step(x, g)
            return c

        lax.fori_loop(0, G, one, 0)

    def pack(r, value):
        def one(g, c):
            acc = [jnp.zeros((8, CY), f32) for _ in range(3)]
            for x in range(CX):
                for f in range(F):
                    put(acc, value(x, f, g), x, f)
            for i in range(3):
                own[r, g, i] = acc[i]
            return c

        lax.fori_loop(0, G, one, 0)

    pl.semaphore_wait(barrier, wanted)
    @pl.when(gx > 0)
    def _():
        for i in range(2):
            send(state.at[:, :, i, :], u0.at[:, CX + 2 + i], 4 * R_U0 + LEFT, 4 * R_U0 + LEFT, {"gx": gx - 1}).start()

    @pl.when(gx < nx - 1)
    def _():
        for i in range(2):
            send(state.at[:, :, CX - 2 + i, :], u0.at[:, i], 4 * R_U0 + RIGHT, 4 * R_U0 + RIGHT, {"gx": gx + 1}).start()

    piece = [(2 * f + h, f, h) for f in range(F) for h in range(2)]

    def fill(block):
        tiles = [jnp.zeros((8, CY), f32), jnp.zeros((8, CY), f32)]
        for i, f, h in piece:
            tiles[i // 8] = tiles[i // 8] + pltpu.roll(block(f, h), CX * (i % 8), 1)
        return tiles

    def unfill(ref, f, h):
        i = 2 * f + h
        return pltpu.roll(ref[i // 8], (CY - CX * (i % 8)) % CY, 1)

    def widen(v):
        wide = jnp.zeros((8, CY), v.dtype)
        for x in range(CX):
            wide = jnp.where(lane == x, v[:, x : x + 1], wide)
        return wide

    here(psn_in, psv, L_PSN).wait()
    for e in range(2):
        psd[e, 0], psd[e, 1] = fill(lambda f, h: widen(psv[e, f, 8 * h : 8 * h + 8]))

        @pl.when(gy == e * (ny - 1))
        def _():
            psn[e * (ny - 1)] = psd[e]

    def signal(sem, axis, to):
        pl.semaphore_signal(sem, inc=1, device_id={axis: jnp.int32(to)}, device_id_type=MESH)

    @pl.when(gy > 0)
    def _():
        signal(above, "gy", gy - 1)
        signal(entered.at[1], "gy", 0)
        send(psd.at[0], psn.at[gy], S_PSN, S_PSN, {"gy": jnp.int32(0)}).start()

    @pl.when(gy == ny - 1)
    def _():
        for i in range(ny - 1):
            signal(opened.at[1], "gy", i)

    @pl.when(west & (gx > 0))
    def _():
        signal(entered.at[0], "gx", 0)

    @pl.when(gx == nx - 1)
    def _():
        for i in range(W - 1, nx - 1, W):
            signal(opened.at[0], "gx", i)

    whole(dp, loc, L_DIF).wait()
    whole(a0, loc, L_COT).wait()

    def first(x, g):
        d = dp[x, rows(g)] * (4.0 / 3.0)
        dp[x, rows(g)] = d
        w = d * ztab[x]
        dz[x, rows(g)] = w
        for f in range(F):
            v = w * a0[f, x, rows(g)]
            q1[f, x + 2, rows(g)] = v

    per_group(range(CX), first)
    pack(R_Q1, lambda x, f, g: q1[f, x + 2, rows(g)])

    ship_x(R_Q1, q1)
    ship_y(R_Q1)
    for e, sub in enumerate(subs):
        @pl.when(gx != sub)
        def _():
            send(pwe_in.at[e], pwe.at[gx], S_PWE + e, S_PWE, {"gx": sub}).start()

        @pl.when(gx == sub)
        def _():
            here(pwe_in.at[e], pwe.at[gx], L_PWE).start()

    whole(u0.at[:, 2 : CX + 2], loc, L_STATE).wait()

    pack(R_U0, lambda x, f, g: u0[f, x + 2, rows(g)])
    ship_y(R_U0)

    here(mix_in, mix, L_MIX).wait()
    taps = [[mix[a, b] * 0.25 + (1.0 if a == b else 0.0) for b in range(F)] for a in range(F)]

    def blend(v, f, back):
        total = (taps[0][f] if back else taps[f][0]) * v[0]
        for g in range(1, F):
            total = total + (taps[g][f] if back else taps[f][g]) * v[g]
        return total

    def retreat(src, q, dst, x, g):
        z = ztab[x]
        p = [z * src[f, x, rows(g)] for f in range(F)]
        for f in range(F):
            t, _ = lap(q, x, f, g)
            dst[f, x, rows(g)] = t + blend(p, f, True)

    def advance(u, dst, shift, x, g):
        z, d = ztab[x], dp[x, rows(g)]
        both = [lap(u, x, f, g) for f in range(F)]
        c = [b[1] for b in both]
        for f in range(F):
            dst[f, x + shift, rows(g)] = z * (d * both[f][0] + blend(c, f, False))

    def sweep(r, ref, step, between=None):
        per_group(INNER, step)
        if between is not None:
            between()
        await_x(r, ref)
        per_group(OUTER, step)

    def block_to(root):
        block = pwe.at[pl.ds(base, W)]
        return send(block, block, S_PWE2, S_PWE2, {"gx": jnp.int32(root)})

    def take_columns():
        for e, sub in enumerate(subs):
            @pl.when(gx == sub)
            def _():
                whole(pwe.at[pl.ds(base + 1 - e, W - 1)], rcv, S_PWE).wait()
                here(pwe_in.at[e], pwe.at[gx], L_PWE).wait()

        @pl.when(west & (gx > 0))
        def _():
            block_to(0).start()

        @pl.when(east & (gx < nx - 1))
        def _():
            pl.semaphore_wait(opened.at[0], 1)
            block_to(nx - 1).start()

    sweep(R_U0, u0, functools.partial(advance, u0, u1, 2))

    middle = gy == ny // 2 - 1
    ship_up(R_Q1, (gy < ny - 1) & jnp.logical_not(middle))
    ship_up(R_U0, (gy < ny - 1) & jnp.logical_not(middle))

    sweep(R_Q1, q1, functools.partial(retreat, a0, q1, mid), take_columns)

    ship_up(R_Q1, middle)
    ship_up(R_U0, middle)

    def send_north(cond):
        @pl.when(cond)
        def _():
            pl.semaphore_wait(opened.at[1], 1)
            send(psd.at[1], psn.at[gy], S_PSN + 1, S_PSN + 1, {"gy": jnp.int32(ny - 1)}).start()

    send_north((gy >= ny // 2 - 1) & (gy < ny - 1))
    await_y(R_Q1)

    def settle_middle(x, f, g):
        m = mid[f, x, rows(g)] + mend(x, f, g)
        mid[f, x, rows(g)] = m
        v = dz[x, rows(g)] * m
        q2[f, x + 2, rows(g)] = v
        return v

    pack(R_Q2, settle_middle)
    ship_x(R_Q2, q2)
    ship_y(R_Q2)
    here(twe_in, twe, L_TWE).wait()
    here(tsn_in, tsn, L_TSN).wait()

    def climb(d, t, width_of):
        arr = jnp.concatenate([d, jnp.zeros((8, width_of), f32)], 0)
        for b in (1, 2, 4):
            arr = jnp.where((t & b)[0:1] != 0, pltpu.roll(arr, b, 0), arr)
        tiles = [arr[8 * j : 8 * j + 8] for j in range(5)]
        for b, size in ((8, 6), (16, 8), (32, 12), (64, 16)):
            on, gap = (t & b) != 0, b // 8
            blank = jnp.zeros((8, width_of), f32)
            take = lambda j: tiles[j] if 0 <= j < len(tiles) else blank
            tiles = [jnp.where(on, take(j - gap), take(j)) for j in range(size)]
        return tiles

    def descend(tiles, t):
        for b, size in ((64, 12), (32, 8), (16, 6), (8, 5)):
            on, gap = (t & b) != 0, b // 8
            tiles = [jnp.where(on, tiles[j + gap], tiles[j]) if j + gap < len(tiles) else tiles[j] for j in range(size)]
        arr = jnp.concatenate(tiles, 0)
        for b in (4, 2, 1):
            arr = jnp.where((t & b)[0:1] != 0, pltpu.roll(arr, 40 - b, 0), arr)
        return arr[0:KC]

    t_we = jnp.broadcast_to(jnp.where(gx == 0, twe[0:1], twe[1:2]), (8, CY))
    t_sn = widen(jnp.broadcast_to(jnp.where(gy == 0, tsn[0:1], tsn[1:2]), (8, CX)))

    @pl.when(x_end)
    def _():
        def one(f, c):
            d = []
            for g in range(G):
                s = xtab[0] * (a0[f, 0, rows(g)] + mid[f, 0, rows(g)])
                for x in range(1, CX):
                    s = s + xtab[x] * (a0[f, x, rows(g)] + mid[f, x, rows(g)])
                d.append(s)
            tiles = climb(jnp.concatenate(d, 0), t_we, CY)
            for j in range(16):
                gw[2 * j, f] = tiles[j][0:4]
                gw[2 * j + 1, f] = tiles[j][4:8]
            return c

        lax.fori_loop(0, F, one, 0)

    @pl.when(y_end)
    def _():
        sums = []
        for f in range(F):
            d = []
            for g in range(G):
                t = jnp.zeros((8, CY), f32)
                for x in range(CX):
                    v = jnp.sum(wy * (a0[f, x, rows(g)] + mid[f, x, rows(g)]), axis=1, keepdims=True)
                    t = jnp.where(lane == x, v, t)
                d.append(t)
            sums.append(climb(jnp.concatenate(d, 0), t_sn, CY))
        for j in range(ny):
            gs[j, 0], gs[j, 1] = fill(lambda f, h: sums[f][2 * j + h])

    def spread_we(e):
        root = e * (nx - 1)
        for j in range(nx // W):
            if j != root // W:
                block = gw.at[pl.ds(j * W, W)]
                send(block, block, S_GWE2, S_GWE2, {"gx": jnp.int32(j * W + e * (W - 1))}).start()

    def spread_sn(e):
        root = e * (ny - 1)
        gsd[e] = gs[root]
        for j in range(ny):
            if j != root:
                send(gs.at[j], gsd.at[e], S_GSN, S_GSN + e, {"gy": jnp.int32(j)}).start()

    for e in range(2):
        @pl.when(gx == e * (nx - 1))
        def _():
            if e == 0:
                pl.semaphore_wait(entered.at[0], nx // W - 1)
            spread_we(e)

        @pl.when(gy == e * (ny - 1))
        def _():
            if e == 0:
                pl.semaphore_wait(entered.at[1], ny - 1)
            spread_sn(e)

    def relay_gradients():
        for e, sub in enumerate(subs):
            @pl.when((gx == sub) & (gx != e * (nx - 1)))
            def _():
                whole(gw.at[pl.ds(base, W)], rcv, S_GWE2).wait()

            @pl.when(gx == sub)
            def _():
                here(gw.at[gx], gwe.at[e], L_GWE).start()
                for j in range(W - 1):
                    to = base + j + 1 - e
                    send(gw.at[to], gwe.at[e], S_GWE, S_GWE + e, {"gx": to}).start()
    send_north((gy < ny // 2 - 1))

    back = functools.partial(retreat, mid, q2, out_g)
    per_group(INNER, back)

    for e in range(2):
        @pl.when(gx == e * (nx - 1))
        def _():
            whole(pwe.at[0 : nx - W] if e else pwe.at[W:nx], rcv, S_PWE2).wait()

        @pl.when(gy == e * (ny - 1))
        def _():
            whole(psn.at[0 : ny - 1] if e else psn.at[1:ny], rcv, S_PSN + e).wait()

    @pl.when(x_end)
    def _():
        def one(f, c):
            tiles = [jnp.concatenate([pwe[2 * j, f], pwe[2 * j + 1, f]], 0) for j in range(16)]
            bwe[f] = descend(tiles, t_we)
            return c

        lax.fori_loop(0, F, one, 0)

    @pl.when(y_end & jnp.logical_not(x_end))
    def _():
        bwe[...] = jnp.zeros((F, KC, CY), f32)

    @pl.when(y_end)
    def _():
        for f in range(F):
            bsn[f] = descend([unfill(psn.at[j // 2], f, j % 2) for j in range(16)], t_sn)

    @pl.when(x_end & jnp.logical_not(y_end))
    def _():
        bsn[...] = jnp.zeros((F, KC, CY), f32)

    @pl.when(x_end | y_end)
    def _():
        def one(f, c):
            b = bsn[f]
            for x in range(CX):
                for g in range(G):
                    v = xtab[x] * bwe[f, rows(g)] + wy * b[8 * g : 8 * g + 8, x : x + 1]
                    edge[f, x, rows(g)] = v
                    u1[f, x + 2, rows(g)] = u1[f, x + 2, rows(g)] + v
            return c

        lax.fori_loop(0, F, one, 0)

    await_y(R_U0)

    def settle_first(x, f, g):
        v = u1[f, x + 2, rows(g)] + dz[x, rows(g)] * mend(x, f, g)
        u1[f, x + 2, rows(g)] = v
        return v

    pack(R_U1, settle_first)
    ship_x(R_U1, u1)
    ship_y(R_U1)

    await_x(R_Q2, q2)
    per_group(OUTER, back)

    relay_gradients()

    sweep(R_U1, u1, functools.partial(advance, u1, out_f, 0))

    @pl.when(x_end | y_end)
    def _():
        def one(f, c):
            for x in range(CX):
                out_f[f, x] = out_f[f, x] + edge[f, x]
            return c

        lax.fori_loop(0, F, one, 0)

    await_y(R_Q2)

    def settle_grad(x, g):
        for f in range(F):
            out_g[f, x, rows(g)] = out_g[f, x, rows(g)] + mend(x, f, g)

    per_group(range(CX), settle_grad)
    await_y(R_U1)

    def settle_final(x, g):
        for f in range(F):
            out_f[f, x, rows(g)] = out_f[f, x, rows(g)] + dz[x, rows(g)] * mend(x, f, g)

    per_group(range(CX), settle_final)

    for r, ref in ((R_Q1, q1), (R_U0, u0), (R_Q2, q2), (R_U1, u1)):
        pair = ref.at[:, 0:2]
        for way, cond, what in (
            (LEFT, gx > 0, pair), (RIGHT, gx < nx - 1, pair),
            (DOWN, gy > 0, packs.at[r, 0]), (UP, gy < ny - 1, packs.at[r, 1]),
        ):
            @pl.when(cond)
            def _():
                whole(what, snd, 4 * r + way).wait()

    for e, sub in enumerate(subs):
        root = e * (nx - 1)

        @pl.when(gx != sub)
        def _():
            whole(pwe_in.at[e], snd, S_PWE + e).wait()
            whole(gwe.at[e], rcv, S_GWE + e).wait()

        @pl.when(gx == sub)
        def _():
            whole(gw.at[pl.ds(base + 1 - e, W - 1)], snd, S_GWE).wait()
            here(gw.at[gx], gwe.at[e], L_GWE).wait()

        @pl.when((gx == sub) & (gx != root))
        def _():
            whole(pwe.at[pl.ds(base, W)], snd, S_PWE2).wait()

        @pl.when(gx == root)
        def _():
            whole(gw.at[0 : nx - W] if e else gw.at[W:nx], snd, S_GWE2).wait()

        last = e * (ny - 1)

        @pl.when(gy != last)
        def _():
            whole(psd.at[e], snd, S_PSN + e).wait()
            whole(gsd.at[e], rcv, S_GSN + e).wait()

        @pl.when(gy == last)
        def _():
            whole(gs.at[0 : ny - 1] if e else gs.at[1:ny], snd, S_GSN).wait()

        for _, f, h in piece:
            gsn[e, f, 8 * h : 8 * h + 8] = unfill(gsd.at[e], f, h)[:, 0:CX]


def store(out_f, out_g, gwe, gsn, final, grad, gwe_out, gsn_out, sems):
    copies = [pltpu.make_async_copy(gwe, gwe_out, sems.at[2]), pltpu.make_async_copy(gsn, gsn_out, sems.at[3])]
    for c in copies:
        c.start()
    for i, (src, dst) in enumerate(((out_f, final), (out_g, grad))):
        for x in range(CX):
            pltpu.make_async_copy(src.at[:, x], dst.at[:, :, x, :], sems.at[i]).start()
        copies.append(pltpu.make_async_copy(src, src, sems.at[i]))
    for c in copies:
        c.wait()


def solution(mesh):
    nx, ny = mesh.shape["gx"], mesh.shape["gy"]
    wide, flat = (F, CX + 4, KC, CY), (F, CX, KC, CY)

    def body(*args):
        far, near = pl.BlockSpec(memory_space=pltpu.HBM), pl.BlockSpec(memory_space=pltpu.VMEM)
        scratch = [wide] * 4 + [flat] * 3 + [
            (CX, KC, CY), (CX, KC, CY), (CX, 8, CY), (CX, 8, CY),
            (nx, F, KP // nx, CY), (2, F, KP // ny, CX), (2, 2, 8, CY), (ny, 2, 8, CY), (F, KC, CY), (F, KC, CY),
            (nx, F, KP // nx, CY), (ny, 2, 8, CY), (2, 2, 8, CY),
            (4, 2, 5, 8, CY), (4, 2, 5, 8, CY), (4, G, 3, 8, CY), (G, 3, 8, CY),
        ]
        child = jax.ShapeDtypeStruct(flat, f32)
        native = jax.ShapeDtypeStruct((F, KC, CX, CY), f32)
        edges = (
            jax.ShapeDtypeStruct((2, F, KP // nx, CY), f32),
            jax.ShapeDtypeStruct((2, F, KP // ny, CX), f32),
        )
        results = pl.pallas_call(
            functools.partial(kernel, nx, ny),
            out_shape=(child, child, *edges),
            in_specs=[far] * 9,
            out_specs=[near] * 4,
            scratch_shapes=[pltpu.VMEM(s, f32) for s in scratch] + [
                pltpu.VMEM((2, CY), jnp.int32),
                pltpu.VMEM((2, CX), jnp.int32),
                pltpu.SMEM((F, F), f32),
                pltpu.VMEM((1, 1), jnp.int32),
                pltpu.SemaphoreType.DMA((10,)),
                pltpu.SemaphoreType.DMA((NSEM,)),
                pltpu.SemaphoreType.DMA((NSEM,)),
                pltpu.SemaphoreType.REGULAR,
                pltpu.SemaphoreType.REGULAR((2,)),
                pltpu.SemaphoreType.REGULAR((2,)),
            ],
            compiler_params=pltpu.CompilerParams(
                collective_id=0, has_side_effects=True, vmem_limit_bytes=VMEM_LIMIT
            ),
            name="nest",
        )(*[pltpu.with_memory_space_constraint(a, pltpu.HBM) for a in args[:8]], args[8].reshape(1, 1))
        return pl.pallas_call(
            store,
            out_shape=(native, native, *edges),
            in_specs=[near] * 4,
            out_specs=[far] * 4,
            scratch_shapes=[pltpu.SemaphoreType.DMA((4,))],
            compiler_params=pltpu.CompilerParams(vmem_limit_bytes=VMEM_LIMIT),
            name="store",
        )(*results)

    return jax.shard_map(
        body,
        mesh=mesh,
        in_specs=(
            P(None, None, "gx", "gy"),
            P(None, None, "gx", "gy"),
            P(None, "gx", "gy"),
            P(),
            P(None, None, "gx", "gy"),
            P(None, None, "gy", "gx"),
            P(None, "gy"),
            P(None, "gx"),
            P(),
        ),
        out_specs=(
            P(None, None, "gx", "gy"),
            P(None, None, "gx", "gy"),
            P(None, None, "gx", "gy"),
            P(None, None, "gy", "gx"),
        ),
        check_vma=False,
    )
```

```python
import functools

import jax
import jax.numpy as jnp
from jax import lax
from jax.experimental import pallas as pl
from jax.experimental.pallas import tpu as pltpu
from jax.sharding import PartitionSpec as P

MESH = pl.DeviceIdType.MESH
F, KC, KP, CX, CY = 5, 32, 128, 16, 128
G = KC // 8
INNER, OUTER = tuple(range(2, CX - 2)), (0, 1, CX - 2, CX - 1)
f32 = jnp.float32

L_COT, L_DIF, L_STATE, L_TWE, L_TSN, L_PWE, L_PSN, L_GWE, L_MIX, L_RW = range(10)
R_Q1, R_U0, R_Q2, R_U1 = range(4)
LEFT, RIGHT, DOWN, UP = range(4)
S_PWE, S_PSN, S_GWE, S_GSN = 16, 18, 20, 22
S_PWE2, S_GWE2 = 24, 25
NSEM = 26
VMEM_LIMIT = 40 * 2**20
W = 8


def tile(shape_dim):
    return lax.broadcasted_iota(jnp.int32, (8, CY), shape_dim)


def kernel(
    nx, ny,
    state, cot, dif, mix_in, pwe_in, psn_in, twe_in, tsn_in, rw_in,
    out_f, out_g, gwe, gsn,
    u0, u1, q1, q2, a0, mid, edge, dp, dz, ztab, xtab,
    pwe, psv, psd, psn, bwe, bsn, gw, gs, gsd, packs, heard, own, halo, twe, tsn, mix, rw,
    loc, snd, rcv, above, opened, entered,
):
    gx, gy = lax.axis_index("gx"), lax.axis_index("gy")
    lane = tile(1)
    low2, high2, quad = lane < 2, lane >= CY - 2, lax.rem(lane, 4) < 2
    ends2 = low2 | high2
    x_end, y_end = (gx == 0) | (gx == nx - 1), (gy == 0) | (gy == ny - 1)

    def here(src, dst, sem):
        return pltpu.make_async_copy(src, dst, loc.at[sem])

    def whole(ref, sems, i):
        return pltpu.make_async_copy(ref, ref, sems.at[i])

    barrier = pltpu.get_barrier_semaphore()

    def greet(cond, to):
        @pl.when(cond)
        def _():
            pl.semaphore_signal(barrier, inc=1, device_id=to, device_id_type=MESH)

    base = gx // W * W
    subs = (base, base + W - 1)
    west, east = gx == subs[0], gx == subs[1]
    both = [(gx > 0, {"gx": gx - 1}), (gx < nx - 1, {"gx": gx + 1})]
    for e, sub in enumerate(subs):
        both.append((gx != sub, {"gx": sub}))
        for j in range(W - 1):
            both.append((gx == sub, {"gx": base + j + 1 - e}))
    told = [(gy < ny - 1, {"gy": gy + 1}), (gy < ny - 1, {"gy": jnp.int32(ny - 1)})]
    told += [(gy == 0, {"gy": jnp.int32(j)}) for j in range(1, ny)]
    told += [(gx == 0, {"gx": jnp.int32(j)}) for j in range(W, nx, W)]
    told += [(east & (gx < nx - 1), {"gx": jnp.int32(nx - 1)})]
    for cond, to in both + told:
        greet(cond, to)
    wanted = sum(cond.astype(jnp.int32) for cond, _ in both)
    wanted = wanted + jnp.where(gy > 0, 2, 0) + jnp.where(gy == ny - 1, ny - 1, 0)
    wanted = wanted + jnp.where(west & (gx > 0), 1, 0) + jnp.where(gx == nx - 1, nx // W - 1, 0)

    here(rw_in, rw, L_RW).start()
    here(psn_in, psv, L_PSN).start()
    for x in range(CX):
        here(cot.at[:, :, x, :], a0.at[:, x], L_COT).start()
        here(dif.at[:, x, :], dp.at[x], L_DIF).start()
    here(mix_in, mix, L_MIX).start()
    for x in range(CX):
        here(state.at[:, :, x, :], u0.at[:, x + 2], L_STATE).start()
    here(twe_in, twe, L_TWE).start()
    here(tsn_in, tsn, L_TSN).start()

    def send(src, dst, i, j, to):
        return pltpu.make_async_remote_copy(src_ref=src, dst_ref=dst, send_sem=snd.at[i], recv_sem=rcv.at[j], device_id=to, device_id_type=MESH)

    def clear(cond, ref, cols):
        @pl.when(cond)
        def _():
            for c in cols:
                for b in ref:
                    b[:, c] = jnp.zeros((F, KC, CY), f32)

    clear(gx == 0, (u0, u1, q1, q2), (0, 1))
    clear(gx == nx - 1, (u0, u1, q1, q2), (CX + 2, CX + 3))

    @pl.when(gy == 0)
    def _():
        heard[:, 0] = jnp.zeros((4, 5, 8, CY), f32)

    @pl.when(gy == ny - 1)
    def _():
        heard[:, 1] = jnp.zeros((4, 5, 8, CY), f32)

    here(rw_in, rw, L_RW).wait()
    width = jnp.broadcast_to(rw[...], (8, CY))
    scale = (width + 1).astype(f32)
    pos_y = gy * CY + lane
    wy = jnp.maximum(width - jnp.minimum(pos_y, ny * CY - 1 - pos_y), 0).astype(f32) / scale

    def wx_of(x):
        pos = gx * CX + x
        return jnp.maximum(width - jnp.minimum(pos, nx * CX - 1 - pos), 0).astype(f32) / scale

    def weights(x, c):
        wx = wx_of(x)
        ztab[x] = (1.0 - wx) * (1.0 - wy)
        xtab[x] = (1.0 - wy) * wx
        return c

    lax.fori_loop(0, CX, weights, 0)

    def rows(g):
        return pl.ds(pl.multiple_of(8 * g, 8), 8)

    def slot(x, f):
        return (0, 8 * x + 4 * f) if f < 2 else (1, 8 * x + 4 * (f - 2) + 2) if f < 4 else (2, 8 * x)

    def put(acc, v, x, f):
        i, p = slot(x, f)
        acc[i] = acc[i] + pltpu.roll(jnp.where(ends2, v, 0.0), (p + 2) % CY, 1)

    def own_of(r, i):
        if i < G:
            return own[r, i, 0], own[r, i, 1]
        return own[r, 0, 2] + pltpu.roll(own[r, 1, 2], 4, 1), pltpu.roll(own[r, 2, 2], 2, 1) + pltpu.roll(own[r, 3, 2], 6, 1)

    def ship_y(r):
        for i in range(5):
            one, two = own_of(r, i)
            packs[r, 1, i] = jnp.where(quad, one, two)
            packs[r, 0, i] = jnp.where(quad, two, one)

        @pl.when(gy > 0)
        def _():
            send(packs.at[r, 0], heard.at[r, 1], 4 * r + DOWN, 4 * r + DOWN, {"gy": gy - 1}).start()

        if r in (R_Q2, R_U1):
            ship_up(r, gy < ny - 1)

    def ship_up(r, cond):
        @pl.when(cond)
        def _():
            if r == R_Q1:
                pl.semaphore_wait(above, 1)
            send(packs.at[r, 1], heard.at[r, 0], 4 * r + UP, 4 * r + UP, {"gy": gy + 1}).start()

    def ship_x(r, ref):
        @pl.when(gx > 0)
        def _():
            send(ref.at[:, 2:4], ref.at[:, CX + 2 : CX + 4], 4 * r + LEFT, 4 * r + LEFT, {"gx": gx - 1}).start()

        @pl.when(gx < nx - 1)
        def _():
            send(ref.at[:, CX : CX + 2], ref.at[:, 0:2], 4 * r + RIGHT, 4 * r + RIGHT, {"gx": gx + 1}).start()

    def await_x(r, ref):
        @pl.when(gx > 0)
        def _():
            whole(ref.at[:, 0:2], rcv, 4 * r + RIGHT).wait()

        @pl.when(gx < nx - 1)
        def _():
            whole(ref.at[:, CX + 2 : CX + 4], rcv, 4 * r + LEFT).wait()

    def await_y(r):
        @pl.when(gy > 0)
        def _():
            whole(heard.at[r, 0], rcv, 4 * r + UP).wait()

        @pl.when(gy < ny - 1)
        def _():
            whole(heard.at[r, 1], rcv, 4 * r + DOWN).wait()

        for i in range(5):
            lo, hi = heard[r, 0, i], heard[r, 1, i]
            mends = []
            for fam, mine in enumerate(own_of(r, i)):
                d = (jnp.where(quad, hi, lo) if fam else jnp.where(quad, lo, hi)) - mine
                place = lax.rem(lane + 2 * fam, 4)
                near = jnp.where(place == 1, pltpu.roll(d, CY - 1, 1), jnp.where(place == 2, pltpu.roll(d, 1, 1), 0.0))
                far = jnp.where(place < 2, pltpu.roll(d, CY - 2, 1), pltpu.roll(d, 2, 1))
                mends.append(near - 0.0625 * far)
            if i < G:
                halo[i, 0], halo[i, 1] = mends
            else:
                halo[0, 2] = mends[0]
                halo[1, 2] = pltpu.roll(mends[0], CY - 4, 1)
                halo[2, 2] = pltpu.roll(mends[1], CY - 2, 1)
                halo[3, 2] = pltpu.roll(mends[1], CY - 6, 1)

    def mend(x, f, g):
        i, p = slot(x, f)
        return jnp.where(ends2, pltpu.roll(halo[g, i], (CY - 2) - p, 1), 0.0)

    def lap(ref, x, f, g):
        c = ref[f, x + 2, rows(g)]
        s1 = pltpu.roll(c, 1, 1) + pltpu.roll(c, CY - 1, 1)
        s2 = pltpu.roll(c, 2, 1) + pltpu.roll(c, CY - 2, 1)
        s1 = s1 + (ref[f, x + 1, rows(g)] + ref[f, x + 3, rows(g)])
        s2 = s2 + (ref[f, x, rows(g)] + ref[f, x + 4, rows(g)])
        return s1 - 0.0625 * s2 - 3.75 * c, c

    def per_group(cols, step):
        def one(g, c):
            for x in cols:
                step(x, g)
            return c

        lax.fori_loop(0, G, one, 0)

    def pack(r, value):
        def one(g, c):
            acc = [jnp.zeros((8, CY), f32) for _ in range(3)]
            for x in range(CX):
                for f in range(F):
                    put(acc, value(x, f, g), x, f)
            for i in range(3):
                own[r, g, i] = acc[i]
            return c

        lax.fori_loop(0, G, one, 0)

    pl.semaphore_wait(barrier, wanted)

    def signal(sem, axis, to):
        pl.semaphore_signal(sem, inc=1, device_id={axis: jnp.int32(to)}, device_id_type=MESH)

    @pl.when(gy > 0)
    def _():
        signal(above, "gy", gy - 1)
        signal(entered.at[1], "gy", 0)

    @pl.when(gy == ny - 1)
    def _():
        for i in range(ny - 1):
            signal(opened.at[1], "gy", i)

    @pl.when(west & (gx > 0))
    def _():
        signal(entered.at[0], "gx", 0)

    @pl.when(gx == nx - 1)
    def _():
        for i in range(W - 1, nx - 1, W):
            signal(opened.at[0], "gx", i)

    @pl.when(gx > 0)
    def _():
        for i in range(2):
            send(state.at[:, :, i, :], u0.at[:, CX + 2 + i], 4 * R_U0 + LEFT, 4 * R_U0 + LEFT, {"gx": gx - 1}).start()

    @pl.when(gx < nx - 1)
    def _():
        for i in range(2):
            send(state.at[:, :, CX - 2 + i, :], u0.at[:, i], 4 * R_U0 + RIGHT, 4 * R_U0 + RIGHT, {"gx": gx + 1}).start()

    whole(dp, loc, L_DIF).wait()
    whole(a0, loc, L_COT).wait()

    def first(x, g):
        d = dp[x, rows(g)] * (4.0 / 3.0)
        dp[x, rows(g)] = d
        w = d * ztab[x]
        dz[x, rows(g)] = w
        for f in range(F):
            v = w * a0[f, x, rows(g)]
            q1[f, x + 2, rows(g)] = v

    per_group(range(CX), first)
    pack(R_Q1, lambda x, f, g: q1[f, x + 2, rows(g)])

    ship_y(R_Q1)
    ship_x(R_Q1, q1)
    for e, sub in enumerate(subs):
        @pl.when(gx != sub)
        def _():
            send(pwe_in.at[e], pwe.at[gx], S_PWE + e, S_PWE, {"gx": sub}).start()

        @pl.when(gx == sub)
        def _():
            here(pwe_in.at[e], pwe.at[gx], L_PWE).start()

    piece = [(2 * f + h, f, h) for f in range(F) for h in range(2)]

    def fill(block):
        tiles = [jnp.zeros((8, CY), f32), jnp.zeros((8, CY), f32)]
        for i, f, h in piece:
            tiles[i // 8] = tiles[i // 8] + pltpu.roll(block(f, h), CX * (i % 8), 1)
        return tiles

    def unfill(ref, f, h):
        i = 2 * f + h
        return pltpu.roll(ref[i // 8], (CY - CX * (i % 8)) % CY, 1)

    def widen(v):
        return jnp.concatenate([v, jnp.zeros((8, CY - CX), v.dtype)], 1)

    here(psn_in, psv, L_PSN).wait()
    for e in range(2):
        psd[e, 0], psd[e, 1] = fill(lambda f, h: widen(psv[e, f, 8 * h : 8 * h + 8]))

        @pl.when(gy == e * (ny - 1))
        def _():
            psn[e * (ny - 1)] = psd[e]

    @pl.when(gy > 0)
    def _():
        send(psd.at[0], psn.at[gy], S_PSN, S_PSN, {"gy": jnp.int32(0)}).start()

    whole(u0.at[:, 2 : CX + 2], loc, L_STATE).wait()

    pack(R_U0, lambda x, f, g: u0[f, x + 2, rows(g)])
    ship_y(R_U0)

    here(mix_in, mix, L_MIX).wait()
    taps = [[mix[a, b] * 0.25 + (1.0 if a == b else 0.0) for b in range(F)] for a in range(F)]

    def blend(v, f, back):
        total = (taps[0][f] if back else taps[f][0]) * v[0]
        for g in range(1, F):
            total = total + (taps[g][f] if back else taps[f][g]) * v[g]
        return total

    def retreat(src, q, dst, x, g):
        z = ztab[x]
        p = [z * src[f, x, rows(g)] for f in range(F)]
        for f in range(F):
            t, _ = lap(q, x, f, g)
            dst[f, x, rows(g)] = t + blend(p, f, True)

    def advance(u, dst, shift, x, g):
        z, d = ztab[x], dp[x, rows(g)]
        both = [lap(u, x, f, g) for f in range(F)]
        c = [b[1] for b in both]
        for f in range(F):
            dst[f, x + shift, rows(g)] = z * (d * both[f][0] + blend(c, f, False))

    def sweep(r, ref, step, between=None):
        per_group(INNER, step)
        if between is not None:
            between()
        await_x(r, ref)
        per_group(OUTER, step)

    def block_to(root):
        block = pwe.at[pl.ds(base, W)]
        return send(block, block, S_PWE2, S_PWE2, {"gx": jnp.int32(root)})

    def take_columns():
        for e, sub in enumerate(subs):
            @pl.when(gx == sub)
            def _():
                whole(pwe.at[pl.ds(base + 1 - e, W - 1)], rcv, S_PWE).wait()
                here(pwe_in.at[e], pwe.at[gx], L_PWE).wait()

        @pl.when(west & (gx > 0))
        def _():
            block_to(0).start()

        @pl.when(east & (gx < nx - 1))
        def _():
            pl.semaphore_wait(opened.at[0], 1)
            block_to(nx - 1).start()

    sweep(R_U0, u0, functools.partial(advance, u0, u1, 2))

    ship_up(R_Q1, gy < ny - 1)
    ship_up(R_U0, gy < ny - 1)

    sweep(R_Q1, q1, functools.partial(retreat, a0, q1, mid), take_columns)

    @pl.when(gy < ny - 1)
    def _():
        pl.semaphore_wait(opened.at[1], 1)
        send(psd.at[1], psn.at[gy], S_PSN + 1, S_PSN + 1, {"gy": jnp.int32(ny - 1)}).start()

    await_y(R_Q1)

    def settle_middle(x, f, g):
        m = mid[f, x, rows(g)] + mend(x, f, g)
        mid[f, x, rows(g)] = m
        v = dz[x, rows(g)] * m
        q2[f, x + 2, rows(g)] = v
        return v

    pack(R_Q2, settle_middle)
    ship_y(R_Q2)
    ship_x(R_Q2, q2)
    here(twe_in, twe, L_TWE).wait()
    here(tsn_in, tsn, L_TSN).wait()

    def climb(d, t, width_of):
        arr = jnp.concatenate([d, jnp.zeros((8, width_of), f32)], 0)
        for b in (1, 2, 4):
            arr = jnp.where((t & b)[0:1] != 0, pltpu.roll(arr, b, 0), arr)
        tiles = [arr[8 * j : 8 * j + 8] for j in range(5)]
        for b, size in ((8, 6), (16, 8), (32, 12), (64, 16)):
            on, gap = (t & b) != 0, b // 8
            blank = jnp.zeros((8, width_of), f32)
            take = lambda j: tiles[j] if 0 <= j < len(tiles) else blank
            tiles = [jnp.where(on, take(j - gap), take(j)) for j in range(size)]
        return tiles

    def descend(tiles, t):
        for b, size in ((64, 12), (32, 8), (16, 6), (8, 5)):
            on, gap = (t & b) != 0, b // 8
            tiles = [jnp.where(on, tiles[j + gap], tiles[j]) if j + gap < len(tiles) else tiles[j] for j in range(size)]
        arr = jnp.concatenate(tiles, 0)
        for b in (4, 2, 1):
            arr = jnp.where((t & b)[0:1] != 0, pltpu.roll(arr, 40 - b, 0), arr)
        return arr[0:KC]

    t_we = jnp.broadcast_to(jnp.where(gx == 0, twe[0:1], twe[1:2]), (8, CY))
    t_sn = widen(jnp.broadcast_to(jnp.where(gy == 0, tsn[0:1], tsn[1:2]), (8, CX)))

    @pl.when(x_end)
    def _():
        def one(f, c):
            d = []
            for g in range(G):
                s = xtab[0] * (a0[f, 0, rows(g)] + mid[f, 0, rows(g)])
                for x in range(1, CX):
                    s = s + xtab[x] * (a0[f, x, rows(g)] + mid[f, x, rows(g)])
                d.append(s)
            tiles = climb(jnp.concatenate(d, 0), t_we, CY)
            for j in range(16):
                gw[2 * j, f] = tiles[j][0:4]
                gw[2 * j + 1, f] = tiles[j][4:8]
            return c

        lax.fori_loop(0, F, one, 0)

    @pl.when(y_end)
    def _():
        sums = []
        for f in range(F):
            d = []
            for g in range(G):
                t = jnp.zeros((8, CY), f32)
                for x in range(CX):
                    v = jnp.sum(wy * (a0[f, x, rows(g)] + mid[f, x, rows(g)]), axis=1, keepdims=True)
                    t = jnp.where(lane == x, v, t)
                d.append(t)
            sums.append(climb(jnp.concatenate(d, 0), t_sn, CY))
        for j in range(ny):
            gs[j, 0], gs[j, 1] = fill(lambda f, h: sums[f][2 * j + h])

    def spread_we(e):
        root = e * (nx - 1)
        for j in range(nx // W):
            if j != root // W:
                block = gw.at[pl.ds(j * W, W)]
                send(block, block, S_GWE2, S_GWE2, {"gx": jnp.int32(j * W + e * (W - 1))}).start()

    def spread_sn(e):
        root = e * (ny - 1)
        gsd[e] = gs[root]
        for j in range(ny):
            if j != root:
                send(gs.at[j], gsd.at[e], S_GSN, S_GSN + e, {"gy": jnp.int32(j)}).start()

    for e in range(2):
        @pl.when(gx == e * (nx - 1))
        def _():
            if e == 0:
                pl.semaphore_wait(entered.at[0], nx // W - 1)
            spread_we(e)

        @pl.when(gy == e * (ny - 1))
        def _():
            if e == 0:
                pl.semaphore_wait(entered.at[1], ny - 1)
            spread_sn(e)

    def relay_gradients():
        for e, sub in enumerate(subs):
            @pl.when((gx == sub) & (gx != e * (nx - 1)))
            def _():
                whole(gw.at[pl.ds(base, W)], rcv, S_GWE2).wait()

            @pl.when(gx == sub)
            def _():
                here(gw.at[gx], gwe.at[e], L_GWE).start()
                for j in range(W - 1):
                    to = base + j + 1 - e
                    send(gw.at[to], gwe.at[e], S_GWE, S_GWE + e, {"gx": to}).start()
    back = functools.partial(retreat, mid, q2, out_g)
    per_group(INNER, back)

    for e in range(2):
        @pl.when(gx == e * (nx - 1))
        def _():
            whole(pwe.at[0 : nx - W] if e else pwe.at[W:nx], rcv, S_PWE2).wait()

        @pl.when(gy == e * (ny - 1))
        def _():
            whole(psn.at[0 : ny - 1] if e else psn.at[1:ny], rcv, S_PSN + e).wait()

    @pl.when(x_end)
    def _():
        def one(f, c):
            tiles = [jnp.concatenate([pwe[2 * j, f], pwe[2 * j + 1, f]], 0) for j in range(16)]
            bwe[f] = descend(tiles, t_we)
            return c

        lax.fori_loop(0, F, one, 0)

    @pl.when(y_end & jnp.logical_not(x_end))
    def _():
        bwe[...] = jnp.zeros((F, KC, CY), f32)

    @pl.when(y_end)
    def _():
        for f in range(F):
            bsn[f] = descend([unfill(psn.at[j // 2], f, j % 2) for j in range(16)], t_sn)

    @pl.when(x_end & jnp.logical_not(y_end))
    def _():
        bsn[...] = jnp.zeros((F, KC, CY), f32)

    @pl.when(x_end | y_end)
    def _():
        def one(f, c):
            b = bsn[f]
            for x in range(CX):
                for g in range(G):
                    v = xtab[x] * bwe[f, rows(g)] + wy * b[8 * g : 8 * g + 8, x : x + 1]
                    edge[f, x, rows(g)] = v
                    u1[f, x + 2, rows(g)] = u1[f, x + 2, rows(g)] + v
            return c

        lax.fori_loop(0, F, one, 0)

    await_y(R_U0)

    def settle_first(x, f, g):
        v = u1[f, x + 2, rows(g)] + dz[x, rows(g)] * mend(x, f, g)
        u1[f, x + 2, rows(g)] = v
        return v

    pack(R_U1, settle_first)
    ship_y(R_U1)
    ship_x(R_U1, u1)

    await_x(R_Q2, q2)
    per_group(OUTER, back)

    relay_gradients()

    sweep(R_U1, u1, functools.partial(advance, u1, out_f, 0))

    @pl.when(x_end | y_end)
    def _():
        def one(f, c):
            for x in range(CX):
                out_f[f, x] = out_f[f, x] + edge[f, x]
            return c

        lax.fori_loop(0, F, one, 0)

    await_y(R_Q2)

    def settle_grad(x, g):
        for f in range(F):
            out_g[f, x, rows(g)] = out_g[f, x, rows(g)] + mend(x, f, g)

    per_group(range(CX), settle_grad)
    await_y(R_U1)

    def settle_final(x, g):
        for f in range(F):
            out_f[f, x, rows(g)] = out_f[f, x, rows(g)] + dz[x, rows(g)] * mend(x, f, g)

    per_group(range(CX), settle_final)

    for r, ref in ((R_Q1, q1), (R_U0, u0), (R_Q2, q2), (R_U1, u1)):
        pair = ref.at[:, 0:2]
        for way, cond, what in (
            (LEFT, gx > 0, pair), (RIGHT, gx < nx - 1, pair),
            (DOWN, gy > 0, packs.at[r, 0]), (UP, gy < ny - 1, packs.at[r, 1]),
        ):
            @pl.when(cond)
            def _():
                whole(what, snd, 4 * r + way).wait()

    for e, sub in enumerate(subs):
        root = e * (nx - 1)

        @pl.when(gx != sub)
        def _():
            whole(pwe_in.at[e], snd, S_PWE + e).wait()
            whole(gwe.at[e], rcv, S_GWE + e).wait()

        @pl.when(gx == sub)
        def _():
            whole(gw.at[pl.ds(base + 1 - e, W - 1)], snd, S_GWE).wait()
            here(gw.at[gx], gwe.at[e], L_GWE).wait()

        @pl.when((gx == sub) & (gx != root))
        def _():
            whole(pwe.at[pl.ds(base, W)], snd, S_PWE2).wait()

        @pl.when(gx == root)
        def _():
            whole(gw.at[0 : nx - W] if e else gw.at[W:nx], snd, S_GWE2).wait()

        last = e * (ny - 1)

        @pl.when(gy != last)
        def _():
            whole(psd.at[e], snd, S_PSN + e).wait()
            whole(gsd.at[e], rcv, S_GSN + e).wait()

        @pl.when(gy == last)
        def _():
            whole(gs.at[0 : ny - 1] if e else gs.at[1:ny], snd, S_GSN).wait()

        for _, f, h in piece:
            gsn[e, f, 8 * h : 8 * h + 8] = unfill(gsd.at[e], f, h)[:, 0:CX]


def store(out_f, out_g, gwe, gsn, final, grad, gwe_out, gsn_out, sems):
    copies = [pltpu.make_async_copy(gwe, gwe_out, sems.at[2]), pltpu.make_async_copy(gsn, gsn_out, sems.at[3])]
    for c in copies:
        c.start()
    for i, (src, dst) in enumerate(((out_f, final), (out_g, grad))):
        for x in range(CX):
            pltpu.make_async_copy(src.at[:, x], dst.at[:, :, x, :], sems.at[i]).start()
        copies.append(pltpu.make_async_copy(src, src, sems.at[i]))
    for c in copies:
        c.wait()


def solution(mesh):
    nx, ny = mesh.shape["gx"], mesh.shape["gy"]
    wide, flat = (F, CX + 4, KC, CY), (F, CX, KC, CY)

    def body(*args):
        far, near = pl.BlockSpec(memory_space=pltpu.HBM), pl.BlockSpec(memory_space=pltpu.VMEM)
        scratch = [wide] * 4 + [flat] * 3 + [
            (CX, KC, CY), (CX, KC, CY), (CX, 8, CY), (CX, 8, CY),
            (nx, F, KP // nx, CY), (2, F, KP // ny, CX), (2, 2, 8, CY), (ny, 2, 8, CY), (F, KC, CY), (F, KC, CY),
            (nx, F, KP // nx, CY), (ny, 2, 8, CY), (2, 2, 8, CY),
            (4, 2, 5, 8, CY), (4, 2, 5, 8, CY), (4, G, 3, 8, CY), (G, 3, 8, CY),
        ]
        child = jax.ShapeDtypeStruct(flat, f32)
        native = jax.ShapeDtypeStruct((F, KC, CX, CY), f32)
        edges = (
            jax.ShapeDtypeStruct((2, F, KP // nx, CY), f32),
            jax.ShapeDtypeStruct((2, F, KP // ny, CX), f32),
        )
        results = pl.pallas_call(
            functools.partial(kernel, nx, ny),
            out_shape=(child, child, *edges),
            in_specs=[far] * 9,
            out_specs=[near] * 4,
            scratch_shapes=[pltpu.VMEM(s, f32) for s in scratch] + [
                pltpu.VMEM((2, CY), jnp.int32),
                pltpu.VMEM((2, CX), jnp.int32),
                pltpu.SMEM((F, F), f32),
                pltpu.VMEM((1, 1), jnp.int32),
                pltpu.SemaphoreType.DMA((10,)),
                pltpu.SemaphoreType.DMA((NSEM,)),
                pltpu.SemaphoreType.DMA((NSEM,)),
                pltpu.SemaphoreType.REGULAR,
                pltpu.SemaphoreType.REGULAR((2,)),
                pltpu.SemaphoreType.REGULAR((2,)),
            ],
            compiler_params=pltpu.CompilerParams(
                collective_id=0, has_side_effects=True, vmem_limit_bytes=VMEM_LIMIT
            ),
            name="nest",
        )(*[pltpu.with_memory_space_constraint(a, pltpu.HBM) for a in args[:8]], args[8].reshape(1, 1))
        return pl.pallas_call(
            store,
            out_shape=(native, native, *edges),
            in_specs=[near] * 4,
            out_specs=[far] * 4,
            scratch_shapes=[pltpu.SemaphoreType.DMA((4,))],
            compiler_params=pltpu.CompilerParams(vmem_limit_bytes=VMEM_LIMIT),
            name="store",
        )(*results)

    return jax.shard_map(
        body,
        mesh=mesh,
        in_specs=(
            P(None, None, "gx", "gy"),
            P(None, None, "gx", "gy"),
            P(None, "gx", "gy"),
            P(),
            P(None, None, "gx", "gy"),
            P(None, None, "gy", "gx"),
            P(None, "gy"),
            P(None, "gx"),
            P(),
        ),
        out_specs=(
            P(None, None, "gx", "gy"),
            P(None, None, "gx", "gy"),
            P(None, None, "gx", "gy"),
            P(None, None, "gy", "gx"),
        ),
        check_vma=False,
    )
```

```python
import functools

import jax
import jax.numpy as jnp
from jax import lax
from jax.experimental import pallas as pl
from jax.experimental.pallas import tpu as pltpu
from jax.sharding import PartitionSpec as P

MESH = pl.DeviceIdType.MESH
F, KC, KP, CX, CY = 5, 32, 128, 16, 128
G = KC // 8
INNER, OUTER = tuple(range(2, CX - 2)), (0, 1, CX - 2, CX - 1)
f32 = jnp.float32

L_COT, L_DIF, L_STATE, L_TWE, L_TSN, L_PWE, L_PSN, L_GWE, L_MIX, L_RW = range(10)
R_Q1, R_U0, R_Q2, R_U1 = range(4)
LEFT, RIGHT, DOWN, UP = range(4)
S_PWE, S_PSN, S_GWE, S_GSN = 16, 18, 20, 22
S_PWE2, S_GWE2 = 24, 25
NSEM = 26
VMEM_LIMIT = 40 * 2**20
W = 8


def tile(shape_dim):
    return lax.broadcasted_iota(jnp.int32, (8, CY), shape_dim)


def kernel(
    nx, ny,
    state, cot, dif, mix_in, pwe_in, psn_in, twe_in, tsn_in, rw_in,
    out_f, out_g, gwe, gsn,
    u0, u1, q1, q2, a0, mid, edge, dp, dz, ztab, xtab,
    pwe, psv, psd, psn, bwe, bsn, gw, gs, gsd, packs, heard, own, halo, twe, tsn, mix, rw,
    loc, snd, rcv, above, opened, entered,
):
    gx, gy = lax.axis_index("gx"), lax.axis_index("gy")
    lane = tile(1)
    low2, high2, quad = lane < 2, lane >= CY - 2, lax.rem(lane, 4) < 2
    ends2 = low2 | high2
    x_end, y_end = (gx == 0) | (gx == nx - 1), (gy == 0) | (gy == ny - 1)

    def here(src, dst, sem):
        return pltpu.make_async_copy(src, dst, loc.at[sem])

    def whole(ref, sems, i):
        return pltpu.make_async_copy(ref, ref, sems.at[i])

    barrier = pltpu.get_barrier_semaphore()

    def greet(cond, to):
        @pl.when(cond)
        def _():
            pl.semaphore_signal(barrier, inc=1, device_id=to, device_id_type=MESH)

    base = gx // W * W
    subs = (base, base + W - 1)
    west, east = gx == subs[0], gx == subs[1]
    both = [(gx > 0, {"gx": gx - 1}), (gx < nx - 1, {"gx": gx + 1})]
    for e, sub in enumerate(subs):
        both.append((gx != sub, {"gx": sub}))
        for j in range(W - 1):
            both.append((gx == sub, {"gx": base + j + 1 - e}))
    told = [(gy < ny - 1, {"gy": gy + 1}), (gy < ny - 1, {"gy": jnp.int32(ny - 1)})]
    told += [(gy == 0, {"gy": jnp.int32(j)}) for j in range(1, ny)]
    told += [(gx == 0, {"gx": jnp.int32(j)}) for j in range(W, nx, W)]
    told += [(east & (gx < nx - 1), {"gx": jnp.int32(nx - 1)})]
    for cond, to in both + told:
        greet(cond, to)
    wanted = sum(cond.astype(jnp.int32) for cond, _ in both)
    wanted = wanted + jnp.where(gy > 0, 2, 0) + jnp.where(gy == ny - 1, ny - 1, 0)
    wanted = wanted + jnp.where(west & (gx > 0), 1, 0) + jnp.where(gx == nx - 1, nx // W - 1, 0)

    here(rw_in, rw, L_RW).start()
    here(psn_in, psv, L_PSN).start()
    for x in range(CX):
        here(cot.at[:, :, x, :], a0.at[:, x], L_COT).start()
        here(dif.at[:, x, :], dp.at[x], L_DIF).start()
    here(mix_in, mix, L_MIX).start()
    for x in range(CX):
        here(state.at[:, :, x, :], u0.at[:, x + 2], L_STATE).start()
    here(twe_in, twe, L_TWE).start()
    here(tsn_in, tsn, L_TSN).start()

    def send(src, dst, i, j, to):
        return pltpu.make_async_remote_copy(src_ref=src, dst_ref=dst, send_sem=snd.at[i], recv_sem=rcv.at[j], device_id=to, device_id_type=MESH)

    def clear(cond, ref, cols):
        @pl.when(cond)
        def _():
            for c in cols:
                for b in ref:
                    b[:, c] = jnp.zeros((F, KC, CY), f32)

    clear(gx == 0, (u0, u1, q1, q2), (0, 1))
    clear(gx == nx - 1, (u0, u1, q1, q2), (CX + 2, CX + 3))

    @pl.when(gy == 0)
    def _():
        heard[:, 0] = jnp.zeros((4, 5, 8, CY), f32)

    @pl.when(gy == ny - 1)
    def _():
        heard[:, 1] = jnp.zeros((4, 5, 8, CY), f32)

    here(rw_in, rw, L_RW).wait()
    width = jnp.broadcast_to(rw[...], (8, CY))
    scale = (width + 1).astype(f32)
    pos_y = gy * CY + lane
    wy = jnp.maximum(width - jnp.minimum(pos_y, ny * CY - 1 - pos_y), 0).astype(f32) / scale

    def wx_of(x):
        pos = gx * CX + x
        return jnp.maximum(width - jnp.minimum(pos, nx * CX - 1 - pos), 0).astype(f32) / scale

    def weights(x, c):
        wx = wx_of(x)
        ztab[x] = (1.0 - wx) * (1.0 - wy)
        xtab[x] = (1.0 - wy) * wx
        return c

    lax.fori_loop(0, CX, weights, 0)

    def rows(g):
        return pl.ds(pl.multiple_of(8 * g, 8), 8)

    def slot(x, f):
        return (0, 8 * x + 4 * f) if f < 2 else (1, 8 * x + 4 * (f - 2) + 2) if f < 4 else (2, 8 * x)

    def put(acc, v, x, f):
        i, p = slot(x, f)
        acc[i] = acc[i] + pltpu.roll(jnp.where(ends2, v, 0.0), (p + 2) % CY, 1)

    def own_of(r, i):
        if i < G:
            return own[r, i, 0], own[r, i, 1]
        return own[r, 0, 2] + pltpu.roll(own[r, 1, 2], 4, 1), pltpu.roll(own[r, 2, 2], 2, 1) + pltpu.roll(own[r, 3, 2], 6, 1)

    def ship_y(r):
        for i in range(5):
            one, two = own_of(r, i)
            packs[r, 1, i] = jnp.where(quad, one, two)
            packs[r, 0, i] = jnp.where(quad, two, one)

        @pl.when(gy > 0)
        def _():
            send(packs.at[r, 0], heard.at[r, 1], 4 * r + DOWN, 4 * r + DOWN, {"gy": gy - 1}).start()

        if r in (R_Q2, R_U1):
            ship_up(r, gy < ny - 1)

    def ship_up(r, cond):
        @pl.when(cond)
        def _():
            if r == R_Q1:
                pl.semaphore_wait(above, 1)
            send(packs.at[r, 1], heard.at[r, 0], 4 * r + UP, 4 * r + UP, {"gy": gy + 1}).start()

    def ship_x(r, ref):
        @pl.when(gx > 0)
        def _():
            send(ref.at[:, 2:4], ref.at[:, CX + 2 : CX + 4], 4 * r + LEFT, 4 * r + LEFT, {"gx": gx - 1}).start()

        @pl.when(gx < nx - 1)
        def _():
            send(ref.at[:, CX : CX + 2], ref.at[:, 0:2], 4 * r + RIGHT, 4 * r + RIGHT, {"gx": gx + 1}).start()

    def await_x(r, ref):
        @pl.when(gx > 0)
        def _():
            whole(ref.at[:, 0:2], rcv, 4 * r + RIGHT).wait()

        @pl.when(gx < nx - 1)
        def _():
            whole(ref.at[:, CX + 2 : CX + 4], rcv, 4 * r + LEFT).wait()

    def await_y(r):
        @pl.when(gy > 0)
        def _():
            whole(heard.at[r, 0], rcv, 4 * r + UP).wait()

        @pl.when(gy < ny - 1)
        def _():
            whole(heard.at[r, 1], rcv, 4 * r + DOWN).wait()

        for i in range(5):
            lo, hi = heard[r, 0, i], heard[r, 1, i]
            mends = []
            for fam, mine in enumerate(own_of(r, i)):
                d = (jnp.where(quad, hi, lo) if fam else jnp.where(quad, lo, hi)) - mine
                place = lax.rem(lane + 2 * fam, 4)
                near = jnp.where(place == 1, pltpu.roll(d, CY - 1, 1), jnp.where(place == 2, pltpu.roll(d, 1, 1), 0.0))
                far = jnp.where(place < 2, pltpu.roll(d, CY - 2, 1), pltpu.roll(d, 2, 1))
                mends.append(near - 0.0625 * far)
            if i < G:
                halo[i, 0], halo[i, 1] = mends
            else:
                halo[0, 2] = mends[0]
                halo[1, 2] = pltpu.roll(mends[0], CY - 4, 1)
                halo[2, 2] = pltpu.roll(mends[1], CY - 2, 1)
                halo[3, 2] = pltpu.roll(mends[1], CY - 6, 1)

    def mend(x, f, g):
        i, p = slot(x, f)
        return jnp.where(ends2, pltpu.roll(halo[g, i], (CY - 2) - p, 1), 0.0)

    def lap(ref, x, f, g):
        c = ref[f, x + 2, rows(g)]
        s1 = pltpu.roll(c, 1, 1) + pltpu.roll(c, CY - 1, 1)
        s2 = pltpu.roll(c, 2, 1) + pltpu.roll(c, CY - 2, 1)
        s1 = s1 + (ref[f, x + 1, rows(g)] + ref[f, x + 3, rows(g)])
        s2 = s2 + (ref[f, x, rows(g)] + ref[f, x + 4, rows(g)])
        return s1 - 0.0625 * s2 - 3.75 * c, c

    def per_group(cols, step):
        def one(g, c):
            for x in cols:
                step(x, g)
            return c

        lax.fori_loop(0, G, one, 0)

    def pack(r, value):
        def one(g, c):
            acc = [jnp.zeros((8, CY), f32) for _ in range(3)]
            for x in range(CX):
                for f in range(F):
                    put(acc, value(x, f, g), x, f)
            for i in range(3):
                own[r, g, i] = acc[i]
            return c

        lax.fori_loop(0, G, one, 0)

    pl.semaphore_wait(barrier, wanted)

    def signal(sem, axis, to):
        pl.semaphore_signal(sem, inc=1, device_id={axis: jnp.int32(to)}, device_id_type=MESH)

    @pl.when(gy > 0)
    def _():
        signal(above, "gy", gy - 1)
        signal(entered.at[1], "gy", 0)

    @pl.when(gy == ny - 1)
    def _():
        for i in range(ny - 1):
            signal(opened.at[1], "gy", i)

    @pl.when(west & (gx > 0))
    def _():
        signal(entered.at[0], "gx", 0)

    @pl.when(gx == nx - 1)
    def _():
        for i in range(W - 1, nx - 1, W):
            signal(opened.at[0], "gx", i)

    @pl.when(gx > 0)
    def _():
        for i in range(2):
            send(state.at[:, :, i, :], u0.at[:, CX + 2 + i], 4 * R_U0 + LEFT, 4 * R_U0 + LEFT, {"gx": gx - 1}).start()

    @pl.when(gx < nx - 1)
    def _():
        for i in range(2):
            send(state.at[:, :, CX - 2 + i, :], u0.at[:, i], 4 * R_U0 + RIGHT, 4 * R_U0 + RIGHT, {"gx": gx + 1}).start()

    whole(dp, loc, L_DIF).wait()
    whole(a0, loc, L_COT).wait()

    def first(x, g):
        d = dp[x, rows(g)] * (4.0 / 3.0)
        dp[x, rows(g)] = d
        w = d * ztab[x]
        dz[x, rows(g)] = w
        for f in range(F):
            v = w * a0[f, x, rows(g)]
            q1[f, x + 2, rows(g)] = v

    per_group(range(CX), first)
    pack(R_Q1, lambda x, f, g: q1[f, x + 2, rows(g)])

    ship_y(R_Q1)
    ship_x(R_Q1, q1)
    for e, sub in enumerate(subs):
        @pl.when(gx != sub)
        def _():
            send(pwe_in.at[e], pwe.at[gx], S_PWE + e, S_PWE, {"gx": sub}).start()

        @pl.when(gx == sub)
        def _():
            here(pwe_in.at[e], pwe.at[gx], L_PWE).start()

    piece = [(2 * f + h, f, h) for f in range(F) for h in range(2)]

    def fill(block):
        tiles = [jnp.zeros((8, CY), f32), jnp.zeros((8, CY), f32)]
        for i, f, h in piece:
            tiles[i // 8] = tiles[i // 8] + pltpu.roll(block(f, h), CX * (i % 8), 1)
        return tiles

    def unfill(ref, f, h):
        i = 2 * f + h
        return pltpu.roll(ref[i // 8], (CY - CX * (i % 8)) % CY, 1)

    def widen(v):
        return jnp.concatenate([v, jnp.zeros((8, CY - CX), v.dtype)], 1)

    here(psn_in, psv, L_PSN).wait()
    for e in range(2):
        psd[e, 0], psd[e, 1] = fill(lambda f, h: widen(psv[e, f, 8 * h : 8 * h + 8]))

        @pl.when(gy == e * (ny - 1))
        def _():
            psn[e * (ny - 1)] = psd[e]

    @pl.when(gy > 0)
    def _():
        send(psd.at[0], psn.at[gy], S_PSN, S_PSN, {"gy": jnp.int32(0)}).start()

    whole(u0.at[:, 2 : CX + 2], loc, L_STATE).wait()

    pack(R_U0, lambda x, f, g: u0[f, x + 2, rows(g)])
    ship_y(R_U0)

    here(mix_in, mix, L_MIX).wait()
    taps = [[mix[a, b] * 0.25 + (1.0 if a == b else 0.0) for b in range(F)] for a in range(F)]

    def blend(v, f, back):
        total = (taps[0][f] if back else taps[f][0]) * v[0]
        for g in range(1, F):
            total = total + (taps[g][f] if back else taps[f][g]) * v[g]
        return total

    def retreat(src, q, dst, x, g):
        z = ztab[x]
        p = [z * src[f, x, rows(g)] for f in range(F)]
        for f in range(F):
            t, _ = lap(q, x, f, g)
            dst[f, x, rows(g)] = t + blend(p, f, True)

    def advance(u, dst, shift, x, g):
        z, d = ztab[x], dp[x, rows(g)]
        both = [lap(u, x, f, g) for f in range(F)]
        c = [b[1] for b in both]
        for f in range(F):
            dst[f, x + shift, rows(g)] = z * (d * both[f][0] + blend(c, f, False))

    def sweep(r, ref, step, between=None):
        per_group(INNER, step)
        if between is not None:
            between()
        await_x(r, ref)
        per_group(OUTER, step)

    def block_to(root):
        block = pwe.at[pl.ds(base, W)]
        return send(block, block, S_PWE2, S_PWE2, {"gx": jnp.int32(root)})

    def take_columns():
        for e, sub in enumerate(subs):
            @pl.when(gx == sub)
            def _():
                whole(pwe.at[pl.ds(base + 1 - e, W - 1)], rcv, S_PWE).wait()
                here(pwe_in.at[e], pwe.at[gx], L_PWE).wait()

        @pl.when(west & (gx > 0))
        def _():
            block_to(0).start()

        @pl.when(east & (gx < nx - 1))
        def _():
            pl.semaphore_wait(opened.at[0], 1)
            block_to(nx - 1).start()

    sweep(R_U0, u0, functools.partial(advance, u0, u1, 2))

    ship_up(R_Q1, gy < ny - 1)
    ship_up(R_U0, gy < ny - 1)

    sweep(R_Q1, q1, functools.partial(retreat, a0, q1, mid), take_columns)

    @pl.when(gy < ny - 1)
    def _():
        pl.semaphore_wait(opened.at[1], 1)
        send(psd.at[1], psn.at[gy], S_PSN + 1, S_PSN + 1, {"gy": jnp.int32(ny - 1)}).start()

    await_y(R_Q1)

    def settle_middle(x, f, g):
        m = mid[f, x, rows(g)] + mend(x, f, g)
        mid[f, x, rows(g)] = m
        v = dz[x, rows(g)] * m
        q2[f, x + 2, rows(g)] = v
        return v

    pack(R_Q2, settle_middle)
    ship_y(R_Q2)
    ship_x(R_Q2, q2)
    here(twe_in, twe, L_TWE).wait()
    here(tsn_in, tsn, L_TSN).wait()

    def climb(d, t, width_of):
        arr = jnp.concatenate([d, jnp.zeros((8, width_of), f32)], 0)
        for b in (1, 2, 4):
            arr = jnp.where((t & b)[0:1] != 0, pltpu.roll(arr, b, 0), arr)
        tiles = [arr[8 * j : 8 * j + 8] for j in range(5)]
        for b, size in ((8, 6), (16, 8), (32, 12), (64, 16)):
            on, gap = (t & b) != 0, b // 8
            blank = jnp.zeros((8, width_of), f32)
            take = lambda j: tiles[j] if 0 <= j < len(tiles) else blank
            tiles = [jnp.where(on, take(j - gap), take(j)) for j in range(size)]
        return tiles

    def descend(tiles, t):
        for b, size in ((64, 12), (32, 8), (16, 6), (8, 5)):
            on, gap = (t & b) != 0, b // 8
            tiles = [jnp.where(on, tiles[j + gap], tiles[j]) if j + gap < len(tiles) else tiles[j] for j in range(size)]
        arr = jnp.concatenate(tiles, 0)
        for b in (4, 2, 1):
            arr = jnp.where((t & b)[0:1] != 0, pltpu.roll(arr, 40 - b, 0), arr)
        return arr[0:KC]

    t_we = jnp.broadcast_to(jnp.where(gx == 0, twe[0:1], twe[1:2]), (8, CY))
    t_sn = widen(jnp.broadcast_to(jnp.where(gy == 0, tsn[0:1], tsn[1:2]), (8, CX)))

    @pl.when(x_end)
    def _():
        def one(f, c):
            d = []
            for g in range(G):
                s = xtab[0] * (a0[f, 0, rows(g)] + mid[f, 0, rows(g)])
                for x in range(1, CX):
                    s = s + xtab[x] * (a0[f, x, rows(g)] + mid[f, x, rows(g)])
                d.append(s)
            tiles = climb(jnp.concatenate(d, 0), t_we, CY)
            for j in range(16):
                gw[2 * j, f] = tiles[j][0:4]
                gw[2 * j + 1, f] = tiles[j][4:8]
            return c

        lax.fori_loop(0, F, one, 0)

    @pl.when(y_end)
    def _():
        sums = []
        for f in range(F):
            d = []
            for g in range(G):
                t = jnp.zeros((8, CY), f32)
                for x in range(CX):
                    v = jnp.sum(wy * (a0[f, x, rows(g)] + mid[f, x, rows(g)]), axis=1, keepdims=True)
                    t = jnp.where(lane == x, v, t)
                d.append(t)
            sums.append(climb(jnp.concatenate(d, 0), t_sn, CY))
        for j in range(ny):
            gs[j, 0], gs[j, 1] = fill(lambda f, h: sums[f][2 * j + h])

    def spread_we(e):
        root = e * (nx - 1)
        for j in range(nx // W):
            if j != root // W:
                block = gw.at[pl.ds(j * W, W)]
                send(block, block, S_GWE2, S_GWE2, {"gx": jnp.int32(j * W + e * (W - 1))}).start()

    def spread_sn(e):
        root = e * (ny - 1)
        gsd[e] = gs[root]
        for j in range(ny):
            if j != root:
                send(gs.at[j], gsd.at[e], S_GSN, S_GSN + e, {"gy": jnp.int32(j)}).start()

    for e in range(2):
        @pl.when(gx == e * (nx - 1))
        def _():
            if e == 0:
                pl.semaphore_wait(entered.at[0], nx // W - 1)
            spread_we(e)

        @pl.when(gy == e * (ny - 1))
        def _():
            if e == 0:
                pl.semaphore_wait(entered.at[1], ny - 1)
            spread_sn(e)

    def relay_gradients():
        for e, sub in enumerate(subs):
            @pl.when((gx == sub) & (gx != e * (nx - 1)))
            def _():
                whole(gw.at[pl.ds(base, W)], rcv, S_GWE2).wait()

            @pl.when(gx == sub)
            def _():
                here(gw.at[gx], gwe.at[e], L_GWE).start()
                for j in range(W - 1):
                    to = base + j + 1 - e
                    send(gw.at[to], gwe.at[e], S_GWE, S_GWE + e, {"gx": to}).start()
    back = functools.partial(retreat, mid, q2, out_g)

    @pl.when(y_end)
    def _():
        per_group(INNER, back)

    for e in range(2):
        @pl.when(gx == e * (nx - 1))
        def _():
            whole(pwe.at[0 : nx - W] if e else pwe.at[W:nx], rcv, S_PWE2).wait()

        @pl.when(gy == e * (ny - 1))
        def _():
            whole(psn.at[0 : ny - 1] if e else psn.at[1:ny], rcv, S_PSN + e).wait()

    @pl.when(x_end)
    def _():
        def one(f, c):
            tiles = [jnp.concatenate([pwe[2 * j, f], pwe[2 * j + 1, f]], 0) for j in range(16)]
            bwe[f] = descend(tiles, t_we)
            return c

        lax.fori_loop(0, F, one, 0)

    @pl.when(y_end & jnp.logical_not(x_end))
    def _():
        bwe[...] = jnp.zeros((F, KC, CY), f32)

    @pl.when(y_end)
    def _():
        for f in range(F):
            bsn[f] = descend([unfill(psn.at[j // 2], f, j % 2) for j in range(16)], t_sn)

    @pl.when(x_end & jnp.logical_not(y_end))
    def _():
        bsn[...] = jnp.zeros((F, KC, CY), f32)

    @pl.when(x_end | y_end)
    def _():
        def one(f, c):
            b = bsn[f]
            for x in range(CX):
                for g in range(G):
                    v = xtab[x] * bwe[f, rows(g)] + wy * b[8 * g : 8 * g + 8, x : x + 1]
                    edge[f, x, rows(g)] = v
                    u1[f, x + 2, rows(g)] = u1[f, x + 2, rows(g)] + v
            return c

        lax.fori_loop(0, F, one, 0)

    await_y(R_U0)

    def settle_first(x, f, g):
        v = u1[f, x + 2, rows(g)] + dz[x, rows(g)] * mend(x, f, g)
        u1[f, x + 2, rows(g)] = v
        return v

    pack(R_U1, settle_first)
    ship_y(R_U1)
    ship_x(R_U1, u1)

    @pl.when(jnp.logical_not(y_end))
    def _():
        per_group(INNER, back)

    await_x(R_Q2, q2)
    per_group(OUTER, back)

    relay_gradients()

    sweep(R_U1, u1, functools.partial(advance, u1, out_f, 0))

    @pl.when(x_end | y_end)
    def _():
        def one(f, c):
            for x in range(CX):
                out_f[f, x] = out_f[f, x] + edge[f, x]
            return c

        lax.fori_loop(0, F, one, 0)

    await_y(R_Q2)

    def settle_grad(x, g):
        for f in range(F):
            out_g[f, x, rows(g)] = out_g[f, x, rows(g)] + mend(x, f, g)

    per_group(range(CX), settle_grad)
    await_y(R_U1)

    def settle_final(x, g):
        for f in range(F):
            out_f[f, x, rows(g)] = out_f[f, x, rows(g)] + dz[x, rows(g)] * mend(x, f, g)

    per_group(range(CX), settle_final)

    for r, ref in ((R_Q1, q1), (R_U0, u0), (R_Q2, q2), (R_U1, u1)):
        pair = ref.at[:, 0:2]
        for way, cond, what in (
            (LEFT, gx > 0, pair), (RIGHT, gx < nx - 1, pair),
            (DOWN, gy > 0, packs.at[r, 0]), (UP, gy < ny - 1, packs.at[r, 1]),
        ):
            @pl.when(cond)
            def _():
                whole(what, snd, 4 * r + way).wait()

    for e, sub in enumerate(subs):
        root = e * (nx - 1)

        @pl.when(gx != sub)
        def _():
            whole(pwe_in.at[e], snd, S_PWE + e).wait()
            whole(gwe.at[e], rcv, S_GWE + e).wait()

        @pl.when(gx == sub)
        def _():
            whole(gw.at[pl.ds(base + 1 - e, W - 1)], snd, S_GWE).wait()
            here(gw.at[gx], gwe.at[e], L_GWE).wait()

        @pl.when((gx == sub) & (gx != root))
        def _():
            whole(pwe.at[pl.ds(base, W)], snd, S_PWE2).wait()

        @pl.when(gx == root)
        def _():
            whole(gw.at[0 : nx - W] if e else gw.at[W:nx], snd, S_GWE2).wait()

        last = e * (ny - 1)

        @pl.when(gy != last)
        def _():
            whole(psd.at[e], snd, S_PSN + e).wait()
            whole(gsd.at[e], rcv, S_GSN + e).wait()

        @pl.when(gy == last)
        def _():
            whole(gs.at[0 : ny - 1] if e else gs.at[1:ny], snd, S_GSN).wait()

        for _, f, h in piece:
            gsn[e, f, 8 * h : 8 * h + 8] = unfill(gsd.at[e], f, h)[:, 0:CX]


def store(out_f, out_g, gwe, gsn, final, grad, gwe_out, gsn_out, sems):
    copies = [pltpu.make_async_copy(gwe, gwe_out, sems.at[2]), pltpu.make_async_copy(gsn, gsn_out, sems.at[3])]
    for c in copies:
        c.start()
    for i, (src, dst) in enumerate(((out_f, final), (out_g, grad))):
        for x in range(CX):
            pltpu.make_async_copy(src.at[:, x], dst.at[:, :, x, :], sems.at[i]).start()
        copies.append(pltpu.make_async_copy(src, src, sems.at[i]))
    for c in copies:
        c.wait()


def solution(mesh):
    nx, ny = mesh.shape["gx"], mesh.shape["gy"]
    wide, flat = (F, CX + 4, KC, CY), (F, CX, KC, CY)

    def body(*args):
        far, near = pl.BlockSpec(memory_space=pltpu.HBM), pl.BlockSpec(memory_space=pltpu.VMEM)
        scratch = [wide] * 4 + [flat] * 3 + [
            (CX, KC, CY), (CX, KC, CY), (CX, 8, CY), (CX, 8, CY),
            (nx, F, KP // nx, CY), (2, F, KP // ny, CX), (2, 2, 8, CY), (ny, 2, 8, CY), (F, KC, CY), (F, KC, CY),
            (nx, F, KP // nx, CY), (ny, 2, 8, CY), (2, 2, 8, CY),
            (4, 2, 5, 8, CY), (4, 2, 5, 8, CY), (4, G, 3, 8, CY), (G, 3, 8, CY),
        ]
        child = jax.ShapeDtypeStruct(flat, f32)
        native = jax.ShapeDtypeStruct((F, KC, CX, CY), f32)
        edges = (
            jax.ShapeDtypeStruct((2, F, KP // nx, CY), f32),
            jax.ShapeDtypeStruct((2, F, KP // ny, CX), f32),
        )
        results = pl.pallas_call(
            functools.partial(kernel, nx, ny),
            out_shape=(child, child, *edges),
            in_specs=[far] * 9,
            out_specs=[near] * 4,
            scratch_shapes=[pltpu.VMEM(s, f32) for s in scratch] + [
                pltpu.VMEM((2, CY), jnp.int32),
                pltpu.VMEM((2, CX), jnp.int32),
                pltpu.SMEM((F, F), f32),
                pltpu.VMEM((1, 1), jnp.int32),
                pltpu.SemaphoreType.DMA((10,)),
                pltpu.SemaphoreType.DMA((NSEM,)),
                pltpu.SemaphoreType.DMA((NSEM,)),
                pltpu.SemaphoreType.REGULAR,
                pltpu.SemaphoreType.REGULAR((2,)),
                pltpu.SemaphoreType.REGULAR((2,)),
            ],
            compiler_params=pltpu.CompilerParams(
                collective_id=0, has_side_effects=True, vmem_limit_bytes=VMEM_LIMIT
            ),
            name="nest",
        )(*[pltpu.with_memory_space_constraint(a, pltpu.HBM) for a in args[:8]], args[8].reshape(1, 1))
        return pl.pallas_call(
            store,
            out_shape=(native, native, *edges),
            in_specs=[near] * 4,
            out_specs=[far] * 4,
            scratch_shapes=[pltpu.SemaphoreType.DMA((4,))],
            compiler_params=pltpu.CompilerParams(vmem_limit_bytes=VMEM_LIMIT),
            name="store",
        )(*results)

    return jax.shard_map(
        body,
        mesh=mesh,
        in_specs=(
            P(None, None, "gx", "gy"),
            P(None, None, "gx", "gy"),
            P(None, "gx", "gy"),
            P(),
            P(None, None, "gx", "gy"),
            P(None, None, "gy", "gx"),
            P(None, "gy"),
            P(None, "gx"),
            P(),
        ),
        out_specs=(
            P(None, None, "gx", "gy"),
            P(None, None, "gx", "gy"),
            P(None, None, "gx", "gy"),
            P(None, None, "gy", "gx"),
        ),
        check_vma=False,
    )
```
